256 devices in a mesh: particle: 16 (over z, core), head: 16 (over x, y).
Axes of the slice: x: 4, y: 4, z: 8, core: 2. Of those that a mesh axis runs over, the one named last changes fastest.
Arguments:
- counts: int32 [128], P('particle'), may hold values from 0 to 8, as said below
- ssm_state: float32 [128, 128, 64, 128], P('particle', 'head'), may hold values from -6 to 6
- conv_value: float32 [128, 3, 8192], P('particle', None, 'head'), may hold values from -6 to 6
- conv_wread: float32 [128, 3, 1024], P('particle'), may hold values from -6 to 6
- token_ids: int32 [128, 4], replicated, may hold values from 0 to 65535
- embedding: bfloat16 [65536, 8192], P('head', 'particle'), may hold values from -6 to 6
- w_gate: bfloat16 [8192, 8192], P('particle', 'head'), may hold values from -0.0625 to 0.0625
- w_value: bfloat16 [8192, 8192], P('particle', 'head'), may hold values from -0.0625 to 0.0625
- w_wread: bfloat16 [8192, 1024], P('particle'), may hold values from -0.0625 to 0.0625
- w_step: bfloat16 [8192, 128], P('particle', 'head'), may hold values from -0.0625 to 0.0625
- kern_value: float32 [4, 8192], P(None, 'head'), may hold values from -0.5 to 0.5
- bias_value: float32 [8192], P('head'), may hold values from -0.5 to 0.5
- kern_wread: float32 [4, 1024], replicated, may hold values from -0.5 to 0.5
- bias_wread: float32 [1024], replicated, may hold values from -0.5 to 0.5
- step_bias: float32 [128], P('head'), may hold values from -4 to -1
- decay_log: float32 [128], P('head'), may hold values from 0 to 2.8
- skip_gain: float32 [128], P('head'), may hold values from 0.5 to 2
- norm_gain: float32 [8192], P('head'), may hold values from 0.5 to 1.5
- w_output: bfloat16 [8192, 8192], P('head', 'particle'), may hold values from -0.0625 to 0.0625
Outputs:
- mixed: bfloat16 [128, 4, 8192], P('head', None, 'particle')
- final_state: float32 [128, 128, 64, 128], P('particle', 'head')
- final_conv: float32 [128, 3, 8192], P('particle', None, 'head')
The draws below stay inside these ranges and needn't reach their ends.
Inputs may be any that keep to these rules, and one draw needn't show every extreme that they name: counts sum to 128; the parent of child j lies between 8 * (j // 8) - 1 and 8 * (j // 8) + 6.
All inputs are finite; a program needn't handle non-finite values.
Results may differ from the reference program's by a relative error of at most 0.02.
Values may be sent and summed in bfloat16 or wider, within the bound.
A program may use at most 64 MiB of HBM per device.

```python
import jax
import jax.numpy as jnp
from jax import lax

D = 8192
HEADS = 128
HEADDIM = 64
STATE = 128
GROUPS = 4
CONV = 4
VOCAB = 65536
STEPS = 4
P_DEV = 8
PARTICLES = 128
INNER = 8192
BCW = 1024


def draw_counts(key, part):
    key = jax.random.fold_in(key, 7)
    key_pick, key_forced = jax.random.split(key, 2)
    group = P_DEV
    total = PARTICLES
    position = jnp.arange(total, dtype=jnp.int32)
    block = position // group
    lowest = jnp.maximum(block * group - 1, 0)
    highest = block * group + group - 1
    offsets = jax.random.randint(key_pick, (total,), 0, 1048576) % (highest - lowest)
    forced = jax.random.randint(key_forced, (), 1, total // group)
    leading = position % group == 0
    offsets = jnp.where(jnp.logical_or(leading, block == forced), 0, offsets)
    parents = (lowest + offsets).astype(jnp.int32)
    return jnp.sum((parents[None, :] == position[:, None]).astype(jnp.int32), axis=1).astype(jnp.int32)


def set_ends(array, key, low, largest):
    longest = array.shape.index(max(array.shape))
    spots = []
    for shift in (0, 1):
        where = [jax.random.randint(jax.random.fold_in(key, axis), (), 0, length) for axis, length in enumerate(array.shape)]
        where[longest] = (where[longest] + shift) % array.shape[longest]
        spots.append(tuple(where))
    return array.at[spots[0]].set(low).at[spots[1]].set(largest)


def steps_of(rng, dims, cuts, smallest, largest):
    gain, own = 1.0, jax.random.fold_in(rng, 6)
    for axis_at, blocks in cuts:
        steps = jnp.exp(jax.random.uniform(jax.random.fold_in(own, axis_at), (blocks,), jnp.float32, smallest / len(cuts), largest / len(cuts)))
        gain = gain * jnp.repeat(steps, dims[axis_at] // blocks).reshape([-1 if axis == axis_at else 1 for axis in range(len(dims))])
    return gain


def normal_values(key, dims, spread, most, cuts=(), kind=jnp.bfloat16):
    loudness = steps_of(key, dims, cuts, -0.22, 0.18) if cuts else 1.0
    values = jax.random.normal(key, dims, jnp.float32) * spread * loudness
    return jnp.minimum(jnp.maximum(values, -most), most).astype(kind)


def setup_inputs(seed: int = 0) -> dict:
    arg_keys = jax.random.split(jax.random.key(seed), 20)
    counts = draw_counts(jax.random.fold_in(arg_keys[19], 71), 0)
    ssm_state = normal_values(arg_keys[1], (PARTICLES, HEADS, HEADDIM, STATE), 1.0, 6.0, ((0, 16), (1, 16)), jnp.float32)
    conv_value = normal_values(arg_keys[2], (PARTICLES, CONV - 1, INNER), 1.0, 6.0, ((0, 16), (2, 16)), jnp.float32)
    conv_wread = normal_values(arg_keys[3], (PARTICLES, CONV - 1, BCW), 1.0, 6.0, ((0, 16),), jnp.float32)
    token_ids = set_ends(jax.random.randint(arg_keys[4], (PARTICLES, STEPS), 0, VOCAB), jax.random.fold_in(arg_keys[4], 1), 0, VOCAB - 1).astype(jnp.int32)
    embedding = normal_values(arg_keys[5], (VOCAB, D), 1.0, 6.0, ((0, 16), (1, 16)))
    w_gate = normal_values(arg_keys[6], (D, INNER), D ** -0.5, 0.0625, ((0, 16), (1, 16)))
    w_value = normal_values(arg_keys[7], (D, INNER), D ** -0.5, 0.0625, ((0, 16), (1, 16)))
    w_wread = normal_values(arg_keys[8], (D, BCW), D ** -0.5, 0.0625, ((0, 16),))
    w_step = normal_values(arg_keys[9], (D, HEADS), D ** -0.5, 0.0625, ((0, 16), (1, 16)))
    kern_value = jnp.clip(jax.random.uniform(arg_keys[10], (CONV, INNER), jnp.float32, -0.5, 0.5) * steps_of(arg_keys[10], (CONV, INNER), ((1, 16),), -0.4, 0.0), -0.5, 0.5)
    bias_value = jnp.clip(jax.random.uniform(arg_keys[11], (INNER,), jnp.float32, -0.5, 0.5) * steps_of(arg_keys[11], (INNER,), ((0, 16),), -0.4, 0.0), -0.5, 0.5)
    kern_wread = jnp.clip(jax.random.uniform(arg_keys[12], (CONV, BCW), jnp.float32, -0.5, 0.5), -0.5, 0.5)
    bias_wread = jnp.clip(jax.random.uniform(arg_keys[13], (BCW,), jnp.float32, -0.5, 0.5), -0.5, 0.5)
    step_bias = jnp.clip(-4.0 + 3.0 * jax.random.uniform(arg_keys[14], (HEADS,), jnp.float32) ** steps_of(arg_keys[14], (HEADS,), ((0, 16),), -0.2, 0.2), -4.0, -1.0)
    decay_log = jnp.clip(2.8 * jax.random.uniform(arg_keys[15], (HEADS,), jnp.float32) ** steps_of(arg_keys[15], (HEADS,), ((0, 16),), -0.2, 0.2), 0.0, 2.8)
    skip_gain = jnp.clip(0.5 + 1.5 * jax.random.uniform(arg_keys[16], (HEADS,), jnp.float32) ** steps_of(arg_keys[16], (HEADS,), ((0, 16),), -0.2, 0.2), 0.5, 2.0)
    norm_gain = jnp.clip(1.0 + 0.1 * jax.random.normal(arg_keys[17], (INNER,), jnp.float32), 0.5, 1.5)
    w_output = normal_values(arg_keys[18], (INNER, D), INNER ** -0.5, 0.0625, ((0, 16), (1, 16)))
    return dict(counts=counts, ssm_state=ssm_state, conv_value=conv_value, conv_wread=conv_wread, token_ids=token_ids, embedding=embedding, w_gate=w_gate, w_value=w_value, w_wread=w_wread, w_step=w_step, kern_value=kern_value, bias_value=bias_value, kern_wread=kern_wread, bias_wread=bias_wread, step_bias=step_bias, decay_log=decay_log, skip_gain=skip_gain, norm_gain=norm_gain, w_output=w_output)


EPSILON = 1e-05

def convolve(history, current, kernel, offset):
    window = jnp.concatenate([history, current[:, None, :].astype(jnp.float32)], axis=1)
    result = jax.nn.silu(lax.optimization_barrier(jnp.sum(window * kernel[None], axis=1)) + offset[None])
    return (result, window[:, 1:])

def reference(counts, ssm_state, conv_value, conv_wread, token_ids, embedding, w_gate, w_value, w_wread, w_step, kern_value, bias_value, kern_wread, bias_wread, step_bias, decay_log, skip_gain, norm_gain, w_output):
    inclusive = jnp.cumsum(counts).astype(jnp.int32)
    children = jnp.arange(PARTICLES, dtype=jnp.int32)
    parents = lax.optimization_barrier(jnp.sum((inclusive[None, :] <= children[:, None]).astype(jnp.int32), axis=1)).astype(jnp.int32)
    states = jnp.take(ssm_state, parents, axis=0)
    value_hist = jnp.take(conv_value, parents, axis=0)
    wread_hist = jnp.take(conv_wread, parents, axis=0)
    tokens = jnp.take(embedding, token_ids.reshape(-1).astype(jnp.int32), axis=0)

    def project(weight):
        product = jnp.dot(tokens, weight, preferred_element_type=jnp.float32).astype(jnp.bfloat16)
        return product.reshape(PARTICLES, STEPS, weight.shape[1])
    gate = project(w_gate)
    value = project(w_value)
    wread = project(w_wread)
    rates = project(w_step)
    repeats = HEADS // GROUPS
    outputs = []
    for moment in range(STEPS):
        value_conv, value_hist = convolve(value_hist, value[:, moment], kern_value, bias_value)
        wread_conv, wread_hist = convolve(wread_hist, wread[:, moment], kern_wread, bias_wread)
        writes = jnp.repeat(wread_conv[:, :GROUPS * STATE].reshape(PARTICLES, GROUPS, STATE), repeats, axis=1)
        reads = jnp.repeat(wread_conv[:, GROUPS * STATE:].reshape(PARTICLES, GROUPS, STATE), repeats, axis=1)
        step_size = jax.nn.softplus(rates[:, moment].astype(jnp.float32) + step_bias[None])
        decay = jnp.exp(-step_size * jnp.exp(decay_log)[None])
        inputs = value_conv.reshape(PARTICLES, HEADS, HEADDIM)
        states = states * decay[:, :, None, None] + (step_size[:, :, None] * inputs)[:, :, :, None] * writes[:, :, None, :]
        reading = lax.optimization_barrier(jnp.sum(states * reads[:, :, None, :], axis=3)) + skip_gain[None, :, None] * inputs
        outputs.append(reading.reshape(PARTICLES, INNER))
    mixer = jnp.stack(outputs, axis=1)
    gated = mixer * jax.nn.silu(gate.astype(jnp.float32))
    grouped = gated.reshape(PARTICLES, STEPS, GROUPS, INNER // GROUPS)
    meansq = lax.optimization_barrier(jnp.mean(grouped * grouped, axis=3))
    normed = (grouped * lax.rsqrt(meansq + EPSILON)[..., None]).reshape(PARTICLES, STEPS, INNER) * norm_gain
    normed = normed.astype(jnp.bfloat16).reshape(PARTICLES * STEPS, INNER)
    mixed = jnp.dot(normed, w_output, preferred_element_type=jnp.float32).astype(jnp.bfloat16)
    return (mixed.reshape(PARTICLES, STEPS, D), states, value_hist)
```

```python
import functools

import jax
import jax.numpy as jnp
from jax import lax
from jax.experimental import pallas as pl
from jax.experimental.pallas import tpu as pltpu
from jax.sharding import PartitionSpec as P

GROUPS = 4
EPSILON = 1e-05
MESH = pl.DeviceIdType.MESH
F32 = jnp.float32
BF16 = jnp.bfloat16
LANES = 128
EMB_PIECES = 4


def silu(x):
    return x * (1.0 / (1.0 + jnp.exp(-x)))


def softplus(x):
    return jnp.maximum(x, 0.0) + jnp.log1p(jnp.exp(-jnp.abs(x)))


def iota(shape, axis):
    return lax.broadcasted_iota(jnp.int32, shape, axis)


def fused(
    np_,
    nh,
    counts,
    step_bias,
    decay_log,
    skip_gain,
    tok,
    kern_value,
    bias_value,
    kern_wread,
    bias_wread,
    norm_gain,
    ssm,
    conv_value,
    conv_wread,
    emb,
    w_gate,
    w_value,
    w_wread,
    w_step,
    w_output,
    mixed,
    final_state,
    final_conv,
    emb_v,
    wg_v,
    wv_v,
    ww_v,
    ws_v,
    wo_v,
    win,
    cwin,
    wwin,
    kw_v,
    sbf,
    fin,
    hist,
    whist,
    tok_part,
    tok_recv,
    tok_all,
    pv,
    pg,
    sv,
    sg,
    sendv_p,
    recvv_p,
    sendv_m,
    recvv_m,
    sendg_p,
    recvg_p,
    sendg_m,
    recvg_m,
    ss_own,
    ss_recv,
    nrm_all,
    part,
    part_recv,
    emb_sem,
    loc_sem,
    shift_send,
    shift_recv,
    rs_send,
    rs_recv,
    ag_send,
    ag_recv,
    sib_send,
    sib_recv,
    ring_send,
    ring_recv,
    ss_send,
    ss_rsem,
    nrm_send,
    nrm_recv,
    fwd_send,
    fwd_recv,
    out_send,
    out_recv,
    fin_sem,
):
    p = lax.axis_index("particle")
    h = lax.axis_index("head")
    zs = np_ // 2
    z = p // 2
    c = p % 2
    sibling = z * 2 + 1 - c
    kids = counts.shape[0]
    steps = tok.shape[1]
    own = kids * steps
    rows = np_ * own
    owned = rows // nh
    width = wv_v.shape[1]
    state = ssm.shape[3]
    heads = ssm.shape[1]
    headdim = ssm.shape[2]
    vocab = emb.shape[0]
    wide = width + 2 * state + LANES
    span = nh // GROUPS
    group = h // span

    barrier = pltpu.get_barrier_semaphore()

    def greet_head(j, _):
        pl.semaphore_signal(
            barrier, inc=1, device_id={"head": lax.rem(h + j, nh)}, device_id_type=MESH
        )
        return 0

    def greet_particle(j, _):
        pl.semaphore_signal(
            barrier, inc=1, device_id={"particle": lax.rem(p + j, np_)}, device_id_type=MESH
        )
        return 0

    lax.fori_loop(1, nh, greet_head, 0)
    lax.fori_loop(1, np_, greet_particle, 0)

    piece = vocab // EMB_PIECES
    emb_copies = [
        pltpu.make_async_copy(
            emb.at[pl.ds(i * piece, piece)], emb_v.at[pl.ds(i * piece, piece)], emb_sem.at[i]
        )
        for i in range(EMB_PIECES)
    ]
    for copy in emb_copies:
        copy.start()
    at_write = pl.ds(pl.multiple_of(group * state, state), state)
    at_read = pl.ds(pl.multiple_of((GROUPS + group) * state, state), state)
    lo, hi = pl.ds(0, state), pl.ds(state, state)
    pairs = [
        (ssm.at[pl.ds(0, kids - 1)], win.at[pl.ds(1, kids - 1)]),
        (conv_value.at[pl.ds(0, kids - 1)], cwin.at[pl.ds(1, kids - 1)]),
        (conv_wread.at[pl.ds(0, kids - 1), :, at_write], wwin.at[0, pl.ds(1, kids - 1)]),
        (conv_wread.at[pl.ds(0, kids - 1), :, at_read], wwin.at[1, pl.ds(1, kids - 1)]),
        (w_value, wv_v),
        (w_wread.at[:, at_write], ww_v.at[:, lo]),
        (w_wread.at[:, at_read], ww_v.at[:, hi]),
        (w_step, ws_v),
        (kern_wread.at[:, at_write], kw_v.at[:, lo]),
        (kern_wread.at[:, at_read], kw_v.at[:, hi]),
        (w_gate, wg_v),
        (w_output, wo_v),
    ]
    loads = [pltpu.make_async_copy(s, d, loc_sem.at[i]) for i, (s, d) in enumerate(pairs)]
    for copy in loads:
        copy.start()

    pl.semaphore_wait(barrier, nh - 1 + np_ - 1)

    above = lax.rem(p + 1, np_)
    shift_pairs = [
        (ssm.at[kids - 1], win.at[0]),
        (conv_value.at[kids - 1], cwin.at[0]),
        (conv_wread.at[kids - 1, :, at_write], wwin.at[0, 0]),
        (conv_wread.at[kids - 1, :, at_read], wwin.at[1, 0]),
    ]
    shifts = [
        pltpu.make_async_remote_copy(
            src_ref=s,
            dst_ref=d,
            send_sem=shift_send.at[i],
            recv_sem=shift_recv.at[i],
            device_id={"particle": above},
            device_id_type=MESH,
        )
        for i, (s, d) in enumerate(shift_pairs)
    ]
    for copy in shifts:
        copy.start()

    column = jnp.concatenate(
        [
            tok[b * kids : (b + 1) * kids, t : t + 1]
            for b in range(np_)
            for t in range(steps)
        ],
        axis=0,
    ) - h * vocab
    half, half_h = rows // 2, nh // 2

    def rs_copy(dest):
        return pltpu.make_async_remote_copy(
            src_ref=tok_part.at[dest],
            dst_ref=tok_recv.at[h],
            send_sem=rs_send.at[dest],
            recv_sem=rs_recv.at[h],
            device_id={"head": dest},
            device_id_type=MESH,
        )

    for m in range(2):
        ids = column[m * half : (m + 1) * half]
        total = None
        for i in range(EMB_PIECES):
            if m == 0:
                emb_copies[i].wait()
            hot = jnp.where(ids - i * piece == iota((half, piece), 1), 1.0, 0.0).astype(BF16)
            term = jnp.dot(hot, emb_v[pl.ds(i * piece, piece)], preferred_element_type=F32)
            total = term if total is None else total + term
        tok_part[pl.ds(m * half_h, half_h)] = total.astype(BF16).reshape(half_h, owned, -1)

        def send_rows(j, _, m=m):
            dest = m * half_h + lax.rem(h + j, half_h)

            @pl.when(dest != h)
            def _():
                rs_copy(dest).start()

            return 0

        lax.fori_loop(0, half_h, send_rows, 0)

    counted = counts[0]
    for i in range(1, kids - 1):
        counted = counted + counts[i]
    running = kids - counted
    marks = [running]
    for i in range(kids - 2):
        running = running + counts[i]
        marks.append(running)
    marks.append(running + counts[kids - 2])
    parent = []
    for k in range(kids):
        at = jnp.int32(0)
        for mark in marks:
            at = at + (mark <= k).astype(jnp.int32)
        parent.append(jnp.minimum(at, kids - 1))
    for copy in loads[:4]:
        copy.wait()
    for copy in shifts:
        copy.wait_recv()
    for k in range(kids):
        sbf[:, pl.ds(k * state, state)] = win[parent[k]].reshape(width, state).astype(BF16)
        picked = cwin[parent[k]]
        for tap in range(3):
            hist[tap, pl.ds(k, 1), :] = picked[tap : tap + 1]
        for side in range(2):
            picked = wwin[side, parent[k]]
            for tap in range(3):
                whist[tap, pl.ds(k, 1), pl.ds(side * state, state)] = picked[tap : tap + 1]

    def rs_wait(s, _):
        @pl.when(s != h)
        def _():
            pltpu.make_async_remote_copy(
                src_ref=tok_part.at[s],
                dst_ref=tok_recv.at[s],
                send_sem=rs_send.at[s],
                recv_sem=rs_recv.at[s],
                device_id={"head": s},
                device_id_type=MESH,
            ).wait()

        return 0

    tok_recv[h] = tok_part[h]
    lax.fori_loop(0, nh, rs_wait, 0)
    shared = tok_recv[0]
    for s in range(1, nh):
        shared = shared + tok_recv[s]
    tok_all[h] = shared

    def ag_copy(j, slot):
        return pltpu.make_async_remote_copy(
            src_ref=tok_all.at[h],
            dst_ref=tok_all.at[h],
            send_sem=ag_send.at[slot],
            recv_sem=ag_recv.at[slot],
            device_id={"head": lax.rem(h + j, nh)},
            device_id_type=MESH,
        )

    def ag_start(j, _):
        ag_copy(j, j).start()
        return 0

    def ag_wait(j, _):
        source = lax.rem(h + nh - j, nh)
        pltpu.make_async_remote_copy(
            src_ref=tok_all.at[h],
            dst_ref=tok_all.at[source],
            send_sem=ag_send.at[j],
            recv_sem=ag_recv.at[j],
            device_id={"head": source},
            device_id_type=MESH,
        ).wait()
        return 0

    lax.fori_loop(1, nh, ag_start, 0)
    for copy in loads[4:]:
        copy.wait()
    lax.fori_loop(1, nh, ag_wait, 0)

    tokens = tok_all[...].reshape(rows, -1)
    reach = zs // 2
    order = [reach]
    for d in range(reach - 1, 0, -1):
        order += [d, -d]
    order.append(0)

    def chip(d):
        return lax.rem(z + d + zs, zs)

    def sib_copy(source, target, kind, i):
        at = chip(order[i])
        return pltpu.make_async_remote_copy(
            src_ref=source.at[1 - c, at],
            dst_ref=target.at[at],
            send_sem=sib_send.at[kind, i],
            recv_sem=sib_recv.at[kind, i],
            device_id={"particle": sibling},
            device_id_type=MESH,
        )

    value_part = jnp.dot(tokens, wv_v[...], preferred_element_type=F32).astype(BF16)
    wread_part = jnp.dot(tokens, ww_v[...], preferred_element_type=F32).astype(BF16)
    step_part = jnp.dot(tokens, ws_v[...], preferred_element_type=F32).astype(BF16)
    rest = jnp.zeros((rows, LANES - heads), BF16)
    step_part = jnp.concatenate([step_part, rest], axis=1)
    for b in range(np_):
        at = slice(b * own, (b + 1) * own)
        pv[b % 2, b // 2, :, pl.ds(0, width)] = value_part[at]
        pv[b % 2, b // 2, :, pl.ds(width, 2 * state)] = wread_part[at]
        pv[b % 2, b // 2, :, pl.ds(width + 2 * state, LANES)] = step_part[at]
    for i in range(zs):
        sib_copy(pv, sv, 0, i).start()
    gate_part = jnp.dot(tokens, wg_v[...], preferred_element_type=F32).astype(BF16)
    for b in range(np_):
        pg[b % 2, b // 2] = gate_part[b * own : (b + 1) * own]
    for i in range(zs):
        sib_copy(pg, sg, 1, i).start()

    arrived = set()

    def chip_sum(kind, d):
        d = d if d != -reach else reach
        i = order.index(d)
        source, target = ((pv, sv), (pg, sg))[kind]
        if (kind, i) not in arrived:
            arrived.add((kind, i))
            sib_copy(source, target, kind, i).wait_recv()
        at = chip(d)
        return source[c, at].astype(F32) + target[at].astype(F32)

    streams = [
        (0, 1, reach, sendv_p, recvv_p),
        (0, -1, reach - 1, sendv_m, recvv_m),
        (1, 1, reach - 1, sendg_p, recvg_p),
        (1, -1, reach, sendg_m, recvg_m),
    ]

    def ring_copy(n, s):
        _, way, _, out, back = streams[n]
        return pltpu.make_async_remote_copy(
            src_ref=out.at[s],
            dst_ref=back.at[s],
            send_sem=ring_send.at[n, s],
            recv_sem=ring_recv.at[n, s],
            device_id={"particle": lax.rem(p + 2 * way + np_, np_)},
            device_id_type=MESH,
        )

    for s in range(reach):
        for n, (kind, way, hops, out, back) in enumerate(streams):
            if s >= hops:
                continue
            term = chip_sum(kind, way * (hops - s))
            if s > 0:
                ring_copy(n, s - 1).wait_recv()
                term = term + back[s - 1].astype(F32)
            out[s] = term.astype(BF16)
            ring_copy(n, s).start()

    def ring_total(kind):
        term = chip_sum(kind, 0)
        for n in (2 * kind, 2 * kind + 1):
            hops, back = streams[n][2], streams[n][4]
            if hops > 0:
                ring_copy(n, hops - 1).wait_recv()
                term = term + back[hops - 1].astype(F32)
        return term.astype(BF16)

    summed = ring_total(0)

    def at_step(a, t):
        return a[t * kids : (t + 1) * kids]

    value = summed[:, :width].astype(F32)
    wread = summed[:, width : width + 2 * state].astype(F32)
    spread = (iota((LANES, width), 1) // headdim == iota((LANES, width), 0)).astype(F32)
    rates = jnp.dot(
        summed[:, width + 2 * state :], spread.astype(BF16), preferred_element_type=F32
    )
    lane_head = iota((1, width), 1) // headdim

    def per_head(ref):
        out = jnp.zeros((1, width), F32)
        for i in range(heads):
            out = jnp.where(lane_head == i, ref[i], out)
        return out

    step_size = softplus(rates + per_head(step_bias))
    decay = jnp.exp(-step_size * jnp.exp(per_head(decay_log)))
    skip = per_head(skip_gain)
    kern = kern_value[...]
    kern_w = kw_v[...]
    bias = bias_value[...]
    bias_w = jnp.concatenate([bias_wread[:, at_write], bias_wread[:, at_read]], axis=1)
    seq = [hist[i] for i in range(3)] + [at_step(value, t) for t in range(steps)]
    seq_w = [whist[i] for i in range(3)] + [at_step(wread, t) for t in range(steps)]
    conv, conv_w = [], []
    for t in range(steps):
        a, b = seq[t] * kern[0:1], seq_w[t] * kern_w[0:1]
        for i in range(1, 4):
            a = a + seq[t + i] * kern[i : i + 1]
            b = b + seq_w[t + i] * kern_w[i : i + 1]
        conv.append(silu(a + bias))
        conv_w.append(silu(b + bias_w))
    writes = [a[:, :state] for a in conv_w]
    reads = [a[:, state:] for a in conv_w]

    child = iota((own, state), 0) % kids

    def apart(blocks):
        whole = jnp.concatenate(blocks, axis=0)
        return jnp.concatenate(
            [jnp.where(child == k, whole, 0.0) for k in range(kids)], axis=1
        ).astype(BF16)

    first = lax.dot_general(
        apart(reads), sbf[...], (((1,), (1,)), ((), ())), preferred_element_type=F32
    )
    kept = None
    added = []
    readings = []
    for t in range(steps):
        now = at_step(decay, t)
        kept = now if kept is None else kept * now
        added = [a * now for a in added] + [at_step(step_size, t) * conv[t]]
        reading = kept * at_step(first, t) + skip * conv[t]
        for u in range(t + 1):
            match = jnp.sum(writes[u] * reads[t], axis=1, keepdims=True)
            reading = reading + added[u] * match
        readings.append(reading)
    gate = ring_total(1).astype(F32)
    gated = jnp.concatenate(readings, axis=0) * silu(gate)

    squares = jnp.sum(gated * gated, axis=1, keepdims=True)
    ss_own[...] = jnp.broadcast_to(squares, (own, LANES))

    def ss_copy(j):
        mate = group * span + lax.rem(h + j, span)
        return pltpu.make_async_remote_copy(
            src_ref=ss_own,
            dst_ref=ss_recv.at[j - 1],
            send_sem=ss_send.at[j - 1],
            recv_sem=ss_rsem.at[j - 1],
            device_id={"head": mate},
            device_id_type=MESH,
        )

    for j in range(1, span):
        ss_copy(j).start()
    meansq = ss_own[...]
    for j in range(1, span):
        ss_copy(j).wait_recv()
        meansq = meansq + ss_recv[j - 1]
    scale = lax.rsqrt(meansq[:, :1] / (width * span) + EPSILON)
    normed = (gated * scale * norm_gain[...]).astype(BF16)
    at_row, from_row = iota((own, own), 0), iota((own, own), 1)
    turn = (from_row == (at_row % steps) * kids + at_row // steps).astype(F32).astype(BF16)
    nrm_all[p] = jnp.dot(turn, normed, preferred_element_type=F32).astype(BF16)

    def nrm_copy(at, target, send, recv):
        return pltpu.make_async_remote_copy(
            src_ref=nrm_all.at[at],
            dst_ref=nrm_all.at[at],
            send_sem=send,
            recv_sem=recv,
            device_id={"particle": target},
            device_id_type=MESH,
        )

    def direct(j):
        return nrm_copy(p, lax.rem(p + 2 * j, np_), nrm_send.at[j - 1], nrm_recv.at[j - 1])

    def forward(j):
        at = lax.rem(p + np_ - 2 * j, np_)
        return nrm_copy(at, sibling, fwd_send.at[j], fwd_recv.at[j])

    near = []
    for d in range(1, reach):
        near += [d, zs - d]
    near.append(reach)
    for j in reversed(near):
        direct(j).start()
    forward(0).start()

    adds = lax.dot_general(
        jnp.concatenate(added, axis=0).astype(BF16),
        apart(writes),
        (((0,), (0,)), ((), ())),
        preferred_element_type=F32,
    )
    for k in range(kids):
        for i in range(heads):
            factor = jnp.broadcast_to(
                kept[k : k + 1, i * headdim : i * headdim + 1], (headdim, state)
            )
            fin[k, i] = (
                win[parent[k], i] * factor
                + adds[i * headdim : (i + 1) * headdim, k * state : (k + 1) * state]
            )
    finals = pltpu.make_async_copy(fin, final_state, fin_sem)
    finals.start()
    for i in range(3):
        final_conv[:, i, :] = at_step(value, steps - 3 + i)

    for j in near:
        at = lax.rem(p + np_ - 2 * j, np_)
        nrm_copy(at, sibling, nrm_send.at[j - 1], nrm_recv.at[j - 1]).wait_recv()
        forward(j).start()
    for j in range(zs):
        at = lax.rem(sibling + np_ - 2 * j, np_)
        nrm_copy(at, sibling, fwd_send.at[j], fwd_recv.at[j]).wait_recv()

    product = jnp.dot(
        nrm_all[...].reshape(rows, width), wo_v[...], preferred_element_type=F32
    ).astype(BF16)
    part[...] = product.reshape(nh, owned, -1)

    def out_copy(j):
        dest = lax.rem(h + j, nh)
        return pltpu.make_async_remote_copy(
            src_ref=part.at[dest],
            dst_ref=part_recv.at[j - 1],
            send_sem=out_send.at[j - 1],
            recv_sem=out_recv.at[j - 1],
            device_id={"head": dest},
            device_id_type=MESH,
        )

    def out_start(j, _):
        out_copy(j).start()
        return 0

    def out_wait(j, _):
        out_copy(j).wait()
        return 0

    lax.fori_loop(1, nh, out_start, 0)

    for copy in shifts:
        copy.wait_send()
    for kind, (source, target) in enumerate(((pv, sv), (pg, sg))):
        for i in range(zs):
            sib_copy(source, target, kind, i).wait_send()
    for n in range(4):
        for s in range(streams[n][2]):
            ring_copy(n, s).wait_send()
    for j in range(1, span):
        ss_copy(j).wait_send()
    for j in range(1, zs):
        direct(j).wait_send()
    for j in range(zs):
        forward(j).wait_send()

    lax.fori_loop(1, nh, out_wait, 0)
    answer = part[h].astype(F32)
    for j in range(nh - 1):
        answer = answer + part_recv[j].astype(F32)
    mixed[...] = answer.reshape(mixed.shape).astype(BF16)
    finals.wait()


def on_device(
    np_,
    nh,
    counts,
    ssm_state,
    conv_value,
    conv_wread,
    token_ids,
    embedding,
    w_gate,
    w_value,
    w_wread,
    w_step,
    kern_value,
    bias_value,
    kern_wread,
    bias_wread,
    step_bias,
    decay_log,
    skip_gain,
    norm_gain,
    w_output,
):
    kids, heads, headdim, state = ssm_state.shape
    steps = token_ids.shape[1]
    own = kids * steps
    rows = np_ * own
    owned = rows // nh
    depth, width = w_value.shape
    cols = w_output.shape[1]
    zs = np_ // 2
    reach = zs // 2
    wide = width + 2 * state + LANES
    span = nh // GROUPS
    taps = kern_value.shape[0]
    back = max(reach - 1, 1)
    dma = pltpu.SemaphoreType.DMA
    scratch = [
        pltpu.VMEM(embedding.shape, BF16),
        pltpu.VMEM((depth, width), BF16),
        pltpu.VMEM((depth, width), BF16),
        pltpu.VMEM((depth, 2 * state), BF16),
        pltpu.VMEM((depth, heads), BF16),
        pltpu.VMEM((width, cols), BF16),
        pltpu.VMEM((kids, heads, headdim, state), F32),
        pltpu.VMEM((kids, 3, width), F32),
        pltpu.VMEM((2, kids, 3, state), F32),
        pltpu.VMEM((taps, 2 * state), F32),
        pltpu.VMEM((width, kids * state), BF16),
        pltpu.VMEM((kids, heads, headdim, state), F32),
        pltpu.VMEM((3, kids, width), F32),
        pltpu.VMEM((3, kids, 2 * state), F32),
        pltpu.VMEM((nh, owned, depth), BF16),
        pltpu.VMEM((nh, owned, depth), BF16),
        pltpu.VMEM((nh, owned, depth), BF16),
        pltpu.VMEM((2, zs, own, wide), BF16),
        pltpu.VMEM((2, zs, own, width), BF16),
        pltpu.VMEM((zs, own, wide), BF16),
        pltpu.VMEM((zs, own, width), BF16),
        pltpu.VMEM((reach, own, wide), BF16),
        pltpu.VMEM((reach, own, wide), BF16),
        pltpu.VMEM((back, own, wide), BF16),
        pltpu.VMEM((back, own, wide), BF16),
        pltpu.VMEM((back, own, width), BF16),
        pltpu.VMEM((back, own, width), BF16),
        pltpu.VMEM((reach, own, width), BF16),
        pltpu.VMEM((reach, own, width), BF16),
        pltpu.VMEM((own, LANES), F32),
        pltpu.VMEM((span - 1, own, LANES), F32),
        pltpu.VMEM((np_, own, width), BF16),
        pltpu.VMEM((nh, owned, cols), BF16),
        pltpu.VMEM((nh - 1, owned, cols), BF16),
        dma((EMB_PIECES,)),
        dma((12,)),
        dma((4,)),
        dma((4,)),
        dma((nh,)),
        dma((nh,)),
        dma((nh,)),
        dma((nh,)),
        dma((2, zs)),
        dma((2, zs)),
        dma((4, reach)),
        dma((4, reach)),
        dma((span - 1,)),
        dma((span - 1,)),
        dma((zs - 1,)),
        dma((zs - 1,)),
        dma((zs,)),
        dma((zs,)),
        dma((nh - 1,)),
        dma((nh - 1,)),
        dma,
    ]
    smem = pl.BlockSpec(memory_space=pltpu.SMEM)
    vmem = pl.BlockSpec(memory_space=pltpu.VMEM)
    hbm = pl.BlockSpec(memory_space=pl.ANY)
    return pl.pallas_call(
        functools.partial(fused, np_, nh),
        out_shape=(
            jax.ShapeDtypeStruct((owned // steps, steps, cols), BF16),
            jax.ShapeDtypeStruct(ssm_state.shape, F32),
            jax.ShapeDtypeStruct(conv_value.shape, F32),
        ),
        in_specs=[smem] * 4 + [vmem] * 3 + [hbm] + [vmem] * 2 + [hbm] * 9,
        out_specs=(vmem, hbm, vmem),
        scratch_shapes=scratch,
        compiler_params=pltpu.CompilerParams(
            collective_id=0, has_side_effects=True, vmem_limit_bytes=48 * 1024 * 1024
        ),
    )(
        counts,
        step_bias,
        decay_log,
        skip_gain,
        token_ids,
        kern_value,
        bias_value.reshape(1, -1),
        kern_wread,
        bias_wread.reshape(1, -1),
        norm_gain.reshape(1, -1),
        ssm_state,
        conv_value,
        conv_wread,
        embedding,
        w_gate,
        w_value,
        w_wread,
        w_step,
        w_output,
    )


def solution(mesh):
    return jax.shard_map(
        functools.partial(on_device, mesh.shape["particle"], mesh.shape["head"]),
        mesh=mesh,
        in_specs=(
            P("particle"),
            P("particle", "head", None, None),
            P("particle", None, "head"),
            P("particle", None, None),
            P(),
            P("head", "particle"),
            P("particle", "head"),
            P("particle", "head"),
            P("particle", None),
            P("particle", "head"),
            P(None, "head"),
            P("head"),
            P(),
            P(),
            P("head"),
            P("head"),
            P("head"),
            P("head"),
            P("head", "particle"),
        ),
        out_specs=(
            P("head", None, "particle"),
            P("particle", "head", None, None),
            P("particle", None, "head"),
        ),
        check_vma=False,
    )
```

```python
import functools

import jax
import jax.numpy as jnp
from jax import lax
from jax.experimental import pallas as pl
from jax.experimental.pallas import tpu as pltpu
from jax.sharding import PartitionSpec as P

GROUPS = 4
EPSILON = 1e-05
MESH = pl.DeviceIdType.MESH
F32 = jnp.float32
BF16 = jnp.bfloat16
LANES = 128
EMB_PIECES = 4


def silu(x):
    return x * (1.0 / (1.0 + jnp.exp(-x)))


def softplus(x):
    return jnp.maximum(x, 0.0) + jnp.log1p(jnp.exp(-jnp.abs(x)))


def iota(shape, axis):
    return lax.broadcasted_iota(jnp.int32, shape, axis)


def keep_rows(kids, counts):
    counted = counts[0]
    for i in range(1, kids - 1):
        counted = counted + counts[i]
    running = kids - counted
    marks = [running]
    for i in range(kids - 1):
        running = running + counts[i]
        marks.append(running)
    parent = []
    for k in range(kids):
        at = jnp.int32(0)
        for mark in marks:
            at = at + (mark <= k).astype(jnp.int32)
        parent.append(jnp.minimum(at, kids - 1))
    return parent


def apart(blocks, kids):
    whole = jnp.concatenate(blocks, axis=0)
    child = iota(whole.shape, 0) % kids
    return jnp.concatenate(
        [jnp.where(child == k, whole, 0.0) for k in range(kids)], axis=1
    ).astype(BF16)


def fused(
    np_,
    nh,
    counts_h,
    step_bias_h,
    decay_log_h,
    skip_gain_h,
    tok_h,
    kern_value_h,
    bias_value_h,
    kern_wread,
    bias_wread,
    norm_gain_h,
    ssm,
    conv_value,
    conv_wread,
    emb,
    w_gate,
    w_value,
    w_wread,
    w_step,
    w_output,
    parts_o,
    below_o,
    kept_o,
    added_o,
    writes_o,
    conv_o,
    counts,
    step_bias,
    decay_log,
    skip_gain,
    tok,
    ids_s,
    kern_value,
    bias_value,
    bw_v,
    norm_gain,
    emb_v,
    wg_v,
    wv_v,
    ww_v,
    ws_v,
    wo_v,
    win,
    cwin,
    wwin,
    kw_v,
    sbf,
    hist,
    whist,
    tok_part,
    tok_recv,
    tok_all,
    term_w,
    term_v,
    term_g,
    sib_w,
    sib_v,
    sib_g,
    out_w,
    out_v,
    out_g,
    in_w,
    in_v,
    in_g,
    quarter,
    nrm_all,
    part,
    kept_v,
    added_v,
    writes_v,
    conv_v,
    tok_sem,
    emb_sem,
    loc_sem,
    shift_send,
    shift_recv,
    rs_send,
    rs_recv,
    ag_send,
    ag_recv,
    sib_send,
    sib_recv,
    z_send,
    z_recv,
    mate_send,
    mate_recv,
    nrm_send,
    nrm_recv,
    fwd_send,
    fwd_recv,
    out_send,
    out_recv,
    own_sem,
    res_sem,
):
    p = lax.axis_index("particle")
    h = lax.axis_index("head")
    zs = np_ // 2
    z = p // 2
    c = p % 2
    sibling = z * 2 + 1 - c
    kids = counts.shape[0]
    steps = tok.shape[0]
    own = kids * steps
    rows = np_ * own
    width = wv_v.shape[1]
    state = ssm.shape[3]
    heads = ssm.shape[1]
    headdim = ssm.shape[2]
    vocab = emb.shape[0]
    span = nh // GROUPS
    group, mate = h // span, h % span
    share = 2 * state // span
    half = rows // 2
    owned = half // nh
    reach = zs // 2
    order = [reach]
    for d in range(reach - 1, 0, -1):
        order += [d, -d]
    order.append(0)

    def chip(d):
        return lax.rem(z + d + zs, zs)

    barrier = pltpu.get_barrier_semaphore()

    def greet_head(j, _):
        pl.semaphore_signal(
            barrier, inc=1, device_id={"head": lax.rem(h + j, nh)}, device_id_type=MESH
        )
        return 0

    def greet_particle(j, _):
        pl.semaphore_signal(
            barrier, inc=1, device_id={"particle": lax.rem(p + j, np_)}, device_id_type=MESH
        )
        return 0

    lax.fori_loop(1, nh, greet_head, 0)
    lax.fori_loop(1, np_, greet_particle, 0)

    tok_copy = pltpu.make_async_copy(tok_h, tok, tok_sem)
    tok_copy.start()
    piece = vocab // EMB_PIECES
    emb_copies = [
        pltpu.make_async_copy(
            emb.at[pl.ds(i * piece, piece)], emb_v.at[pl.ds(i * piece, piece)], emb_sem.at[i]
        )
        for i in range(EMB_PIECES)
    ]
    for copy in emb_copies:
        copy.start()
    at_write = pl.ds(pl.multiple_of(group * state, state), state)
    at_read = pl.ds(pl.multiple_of((GROUPS + group) * state, state), state)
    side = mate // (span // 2)
    at_share = pl.ds(pl.multiple_of((side * GROUPS + group) * state, state), state)
    lo, hi = pl.ds(0, state), pl.ds(state, state)
    pairs = [
        (ssm.at[pl.ds(0, kids - 1)], win.at[pl.ds(1, kids - 1)]),
        (conv_value, cwin.at[1]),
        (conv_wread.at[:, :, at_write], wwin.at[1, :, :, lo]),
        (conv_wread.at[:, :, at_read], wwin.at[1, :, :, hi]),
        (counts_h, counts),
        (w_wread.at[:, at_share], ww_v),
        (w_step, ws_v),
        (w_value, wv_v),
        (w_gate, wg_v),
        (kern_wread.at[:, at_write], kw_v.at[:, lo]),
        (kern_wread.at[:, at_read], kw_v.at[:, hi]),
        (w_output, wo_v),
        (step_bias_h, step_bias),
        (decay_log_h, decay_log),
        (skip_gain_h, skip_gain),
        (kern_value_h, kern_value),
        (bias_value_h, bias_value),
        (norm_gain_h, norm_gain),
        (bias_wread.at[:, at_write], bw_v.at[:, lo]),
        (bias_wread.at[:, at_read], bw_v.at[:, hi]),
    ]
    loads = [pltpu.make_async_copy(s, d, loc_sem.at[i]) for i, (s, d) in enumerate(pairs)]
    for copy in loads:
        copy.start()

    tok_copy.wait()
    ids_t = jnp.concatenate([tok[...], jnp.zeros((8 - steps, np_ * kids), jnp.int32)], axis=0).T
    ids_s[...] = ids_t - h * vocab

    def lookup(m):
        column = []
        for d in order[m * reach : (m + 1) * reach]:
            pair = ids_s[pl.ds(pl.multiple_of(chip(d) * 2 * kids, 2 * kids), 2 * kids), :]
            for core in range(2):
                for t in range(steps):
                    column.append(pair[core * kids : (core + 1) * kids, t : t + 1])
        ids = jnp.concatenate(column, axis=0)
        total = None
        for i in range(EMB_PIECES):
            if m == 0:
                emb_copies[i].wait()
            hot = jnp.where(ids - i * piece == iota((half, piece), 1), 1.0, 0.0).astype(BF16)
            term = jnp.dot(hot, emb_v[pl.ds(i * piece, piece)], preferred_element_type=F32)
            total = term if total is None else total + term
        tok_part[m] = total.astype(BF16).reshape(nh, owned, -1)

    def rs_copy(m, j):
        dest = lax.rem(h + j, nh)
        return pltpu.make_async_remote_copy(
            src_ref=tok_part.at[m, dest],
            dst_ref=tok_recv.at[m, j - 1],
            send_sem=rs_send.at[m, j - 1],
            recv_sem=rs_recv.at[m, j - 1],
            device_id={"head": dest},
            device_id_type=MESH,
        )

    def ag_copy(m, j):
        return pltpu.make_async_remote_copy(
            src_ref=tok_all.at[m, h],
            dst_ref=tok_all.at[m, h],
            send_sem=ag_send.at[m, j - 1],
            recv_sem=ag_recv.at[m, j - 1],
            device_id={"head": lax.rem(h + j, nh)},
            device_id_type=MESH,
        )

    def ag_back(m, j):
        source = lax.rem(h + nh - j, nh)
        return pltpu.make_async_remote_copy(
            src_ref=tok_all.at[m, h],
            dst_ref=tok_all.at[m, source],
            send_sem=ag_send.at[m, j - 1],
            recv_sem=ag_recv.at[m, j - 1],
            device_id={"head": source},
            device_id_type=MESH,
        )

    def each(do):
        def step(j, _):
            do(j)
            return 0

        lax.fori_loop(1, nh, step, 0)

    lookup(0)
    pl.semaphore_wait(barrier, nh - 1 + np_ - 1)
    each(lambda j: rs_copy(0, j).start())

    above = lax.rem(p + 1, np_)
    shift_pairs = [
        (ssm.at[kids - 1], win.at[0]),
        (conv_value, cwin.at[0]),
        (conv_wread.at[:, :, at_write], wwin.at[0, :, :, lo]),
        (conv_wread.at[:, :, at_read], wwin.at[0, :, :, hi]),
    ]
    shifts = [
        pltpu.make_async_remote_copy(
            src_ref=s,
            dst_ref=d,
            send_sem=shift_send.at[i],
            recv_sem=shift_recv.at[i],
            device_id={"particle": above},
            device_id_type=MESH,
        )
        for i, (s, d) in enumerate(shift_pairs)
    ]
    for copy in shifts:
        copy.start()
    lookup(1)
    each(lambda j: rs_copy(1, j).start())

    for m in range(2):
        each(lambda j, m=m: rs_copy(m, j).wait_recv())
        shared = tok_part[m, h]
        for s in range(nh - 1):
            shared = shared + tok_recv[m, s]
        tok_all[m, h] = shared
        each(lambda j, m=m: ag_copy(m, j).start())

    for copy in loads[:5]:
        copy.wait()
    parent = keep_rows(kids, counts)
    for copy in shifts:
        copy.wait_recv()
    below = pltpu.make_async_copy(win.at[0], below_o, res_sem.at[0])
    below.start()
    for k in range(kids):
        sbf[:, pl.ds(k * state, state)] = win[parent[k]].reshape(width, state).astype(BF16)
        here = jnp.minimum(parent[k], 1)
        row = pl.ds(jnp.where(parent[k] == 0, kids - 1, parent[k] - 1), 1)
        for tap in range(3):
            hist[tap, pl.ds(k, 1), :] = cwin[here, tap, row, :]
            whist[tap, pl.ds(k, 1), :] = wwin[here, tap, row, :]
    for copy in loads[5:]:
        copy.wait()

    kinds = [
        (term_w, sib_w, out_w, in_w),
        (term_v, sib_v, out_v, in_v),
        (term_g, sib_g, out_g, in_g),
    ]

    def sib_copy(kind, m):
        source, target = kinds[kind][:2]
        return pltpu.make_async_remote_copy(
            src_ref=source.at[1 - c, pl.ds(m * reach, reach)],
            dst_ref=target.at[pl.ds(m * reach, reach)],
            send_sem=sib_send.at[kind, m],
            recv_sem=sib_recv.at[kind, m],
            device_id={"particle": sibling},
            device_id_type=MESH,
        )

    def z_copy(kind, i):
        _, _, out, back = kinds[kind]
        return pltpu.make_async_remote_copy(
            src_ref=out.at[i],
            dst_ref=back.at[i],
            send_sem=z_send.at[kind, i],
            recv_sem=z_recv.at[kind, i],
            device_id={"particle": lax.rem(p + 2 * order[i] + np_, np_)},
            device_id_type=MESH,
        )

    def place(kind, m, terms):
        source = kinds[kind][0]
        for b in range(2 * reach):
            source[b % 2, m * reach + b // 2] = terms[b * own : (b + 1) * own].astype(BF16)
        sib_copy(kind, m).start()

    def chip_sum(kind, i):
        return kinds[kind][0][c, i].astype(F32) + kinds[kind][1][i].astype(F32)

    def send_sums(kind, m):
        sib_copy(kind, m).wait_recv()
        for i in range(m * reach, min((m + 1) * reach, zs - 1)):
            kinds[kind][2][i] = chip_sum(kind, i).astype(BF16)
            z_copy(kind, i).start()

    def arrive(kind):
        total = chip_sum(kind, zs - 1)
        for i in range(zs - 1):
            z_copy(kind, i).wait_recv()
            total = total + kinds[kind][3][i].astype(F32)
        return total.astype(BF16)

    for m in range(2):
        each(lambda j, m=m: ag_back(m, j).wait_recv())
        tokens = tok_all[m].reshape(half, -1)
        matrices = jnp.dot(tokens, ww_v[...], preferred_element_type=F32)
        rate = lax.dot_general(
            tokens, ws_v[...], (((1,), (1,)), ((), ())), preferred_element_type=F32
        )
        pads = [jnp.zeros((half, n), F32) for n in (share, LANES - share - heads)]
        rate = jnp.concatenate([pads[0], rate, pads[1]], axis=1)
        turned = jnp.concatenate([matrices[:, share:], matrices[:, :share]], axis=1)
        matrices = jnp.where(mate % (span // 2) == 0, matrices, turned)
        place(0, m, jnp.where(iota((half, LANES), 1) < share, matrices, rate))
        place(1, m, jnp.dot(tokens, wv_v[...], preferred_element_type=F32))
        place(2, m, jnp.dot(tokens, wg_v[...], preferred_element_type=F32))
        send_sums(0, m)
        send_sums(1, m)
    for m in range(2):
        send_sums(2, m)

    narrow = arrive(0)
    quarter[mate] = narrow

    def mate_copy(j):
        return pltpu.make_async_remote_copy(
            src_ref=quarter.at[mate],
            dst_ref=quarter.at[mate],
            send_sem=mate_send.at[j - 1],
            recv_sem=mate_recv.at[j - 1],
            device_id={"head": group * span + lax.rem(mate + j, span)},
            device_id_type=MESH,
        )

    def mate_back(j):
        source = lax.rem(mate + span - j, span)
        return pltpu.make_async_remote_copy(
            src_ref=quarter.at[mate],
            dst_ref=quarter.at[source],
            send_sem=mate_send.at[j - 1],
            recv_sem=mate_recv.at[j - 1],
            device_id={"head": group * span + source},
            device_id_type=MESH,
        )

    for j in range(1, span):
        mate_copy(j).start()

    def at_step(a, t):
        return a[t * kids : (t + 1) * kids]

    spread = (
        iota((LANES, width), 1) // headdim + share == iota((LANES, width), 0)
    ).astype(F32)
    rates = jnp.dot(narrow, spread.astype(BF16), preferred_element_type=F32)
    lane_head = iota((1, width), 1) // headdim

    def per_head(ref):
        out = jnp.zeros((1, width), F32)
        for i in range(heads):
            out = jnp.where(lane_head == i, ref[i], out)
        return out

    step_size = softplus(rates + per_head(step_bias))
    decay = jnp.exp(-step_size * jnp.exp(per_head(decay_log)))
    skip = per_head(skip_gain)

    def convolve(past, current, kern, bias):
        seq = [past[i] for i in range(3)] + [at_step(current, t) for t in range(steps)]
        out = []
        for t in range(steps):
            a = seq[t] * kern[0:1]
            for i in range(1, 4):
                a = a + seq[t + i] * kern[i : i + 1]
            out.append(silu(a + bias))
        return out

    for j in range(1, span):
        mate_back(j).wait_recv()
    wread = jnp.concatenate([quarter[i].astype(F32)[:, :share] for i in range(span)], axis=1)
    conv_w = convolve(whist, wread, kw_v[...], bw_v[...])
    writes = [a[:, :state] for a in conv_w]
    reads = [a[:, state:] for a in conv_w]
    first = lax.dot_general(
        apart(reads, kids), sbf[...], (((1,), (1,)), ((), ())), preferred_element_type=F32
    )
    value = arrive(1).astype(F32)
    conv = convolve(hist, value, kern_value[...], bias_value[...])

    kept = None
    added = []
    readings = []
    for t in range(steps):
        now = at_step(decay, t)
        kept = now if kept is None else kept * now
        added = [a * now for a in added] + [at_step(step_size, t) * conv[t]]
        reading = kept * at_step(first, t) + skip * conv[t]
        for u in range(t + 1):
            match = jnp.sum(writes[u] * reads[t], axis=1, keepdims=True)
            reading = reading + added[u] * match
        readings.append(reading)
    kept_v[...] = kept
    added_v[...] = jnp.concatenate(added, axis=0)
    writes_v[...] = jnp.concatenate(writes, axis=0)
    for i in range(3):
        conv_v[i] = at_step(value, steps - 3 + i)
    results = [
        pltpu.make_async_copy(s, d, res_sem.at[i + 1])
        for i, (s, d) in enumerate(
            [(kept_v, kept_o), (added_v, added_o), (writes_v, writes_o), (conv_v, conv_o)]
        )
    ]
    for copy in results:
        copy.start()
    gated = jnp.concatenate(readings, axis=0) * silu(arrive(2).astype(F32))

    squares = jnp.sum(gated * gated, axis=1, keepdims=True)
    upper = squares.astype(BF16).astype(F32)
    lane = iota((own, LANES), 1)
    squares = jnp.where(lane % 2 == 0, upper, squares - upper).astype(BF16)
    scaled = jnp.concatenate([(gated * norm_gain[...]).astype(BF16), squares], axis=1)
    at_row, from_row = iota((own, own), 0), iota((own, own), 1)
    turn = (from_row == (at_row % steps) * kids + at_row // steps).astype(F32).astype(BF16)
    scaled = jnp.dot(turn, scaled, preferred_element_type=F32)
    bands, cuts = own // 16, width // LANES
    marks = scaled[:16, width:]
    for r in range(bands):
        band = scaled[r * 16 : (r + 1) * 16]
        for i in range(cuts):
            nrm_all[p, r * cuts + i] = band[:, i * LANES : (i + 1) * LANES].astype(BF16)
        if r > 0:
            marks = jnp.where(iota(marks.shape, 1) < 2 * r, marks, band[:, width:])
    nrm_all[p, bands * cuts] = marks.astype(BF16)

    def nrm_copy(at, target, send, recv):
        return pltpu.make_async_remote_copy(
            src_ref=nrm_all.at[at],
            dst_ref=nrm_all.at[at],
            send_sem=send,
            recv_sem=recv,
            device_id={"particle": target},
            device_id_type=MESH,
        )

    def direct(i):
        target = lax.rem(p + 2 * order[i] + np_, np_)
        return nrm_copy(p, target, nrm_send.at[i], nrm_recv.at[i])

    def forward(i):
        at = lax.rem(p - 2 * order[i] + np_, np_)
        return nrm_copy(at, sibling, fwd_send.at[i], fwd_recv.at[i])

    for i in range(zs - 1):
        direct(i).start()
    forward(zs - 1).start()

    def dest_of(i, core):
        return lax.rem(z - order[i] + zs, zs) * 2 + core

    def out_copy(i, core):
        return pltpu.make_async_remote_copy(
            src_ref=part.at[i, core],
            dst_ref=parts_o.at[h],
            send_sem=out_send.at[i, core],
            recv_sem=out_recv.at[h],
            device_id={"head": dest_of(i, core)},
            device_id_type=MESH,
        )

    def own_copy(i, core):
        return pltpu.make_async_copy(part.at[i, core], parts_o.at[h], own_sem)

    def send_parts(places):
        block = []
        for i in places:
            for core in range(2):
                tiles = nrm_all[dest_of(i, core)]
                for r in range(bands):
                    block.append(
                        jnp.concatenate([tiles[r * cuts + n] for n in range(cuts)], axis=1)
                    )
        product = jnp.dot(
            jnp.concatenate(block, axis=0), wo_v[...], preferred_element_type=F32
        ).astype(BF16)
        for n, i in enumerate(places):
            for core in range(2):
                for r in range(bands):
                    start = (2 * n + core) * own + r * 16
                    for e in range(cuts):
                        part[i, core, r * cuts + e] = product[
                            start : start + 16, e * LANES : (e + 1) * LANES
                        ]
                part[i, core, bands * cuts] = nrm_all[dest_of(i, core), bands * cuts]
        for i in places:
            for core in range(2):
                dest = dest_of(i, core)

                @pl.when(dest != h)
                def _(i=i, core=core):
                    out_copy(i, core).start()

                @pl.when(dest == h)
                def _(i=i, core=core):
                    own_copy(i, core).start()

    def take(i):
        at = lax.rem(p - 2 * order[i] + np_, np_)
        if order[i] != 0:
            nrm_copy(at, sibling, nrm_send.at[i], nrm_recv.at[i]).wait_recv()
            forward(i).start()

    def take_forward(i):
        at = lax.rem(sibling - 2 * order[i] + np_, np_)
        nrm_copy(at, sibling, fwd_send.at[i], fwd_recv.at[i]).wait_recv()

    near = list(range(zs))[::-1]
    batches = [near[: max(1, zs // 2 - 1)], near[max(1, zs // 2 - 1) :]]
    for batch in batches:
        for i in batch:
            take(i)
        for i in batch:
            take_forward(i)
        send_parts(batch)

    for m in range(2):
        each(lambda j, m=m: rs_copy(m, j).wait_send())
        each(lambda j, m=m: ag_copy(m, j).wait_send())
    for copy in shifts:
        copy.wait_send()
    for kind in range(3):
        for m in range(2):
            sib_copy(kind, m).wait_send()
        for i in range(zs - 1):
            z_copy(kind, i).wait_send()
    for j in range(1, span):
        mate_copy(j).wait_send()
    for i in range(zs - 1):
        direct(i).wait_send()
    for i in range(zs):
        forward(i).wait_send()
    below.wait()
    for copy in results:
        copy.wait()
    for i in range(zs):
        for core in range(2):
            dest = dest_of(i, core)

            @pl.when(dest != h)
            def _(i=i, core=core):
                out_copy(i, core).wait_send()

    own_copy(0, 0).wait()

    def out_wait(s, _):
        @pl.when(s != h)
        def _():
            pltpu.make_async_remote_copy(
                src_ref=part.at[0, 0],
                dst_ref=parts_o.at[s],
                send_sem=out_send.at[0, 0],
                recv_sem=out_recv.at[s],
                device_id={"head": s},
                device_id_type=MESH,
            ).wait_recv()

        return 0

    lax.fori_loop(0, nh, out_wait, 0)


def finish(
    nh,
    parts_h,
    below_h,
    kept_h,
    added_h,
    writes_h,
    conv_h,
    counts_h,
    ssm,
    mixed,
    final_state,
    final_conv,
    parts,
    kept,
    added,
    writes,
    counts,
    win,
    fin,
    load_sem,
    win_sem,
    out_sem,
):
    kids, heads, headdim, state = final_state.shape
    own = added.shape[0]
    steps = own // kids
    width = heads * headdim
    span = nh // GROUPS
    pairs = [
        (counts_h, counts),
        (kept_h, kept),
        (added_h, added),
        (writes_h, writes),
        (below_h, win.at[0]),
        (ssm.at[pl.ds(0, kids - 1)], win.at[pl.ds(1, kids - 1)]),
        (parts_h, parts),
        (conv_h, final_conv),
    ]
    loads = [pltpu.make_async_copy(s, d, load_sem.at[i]) for i, (s, d) in enumerate(pairs)]
    for copy in loads:
        copy.start()
    for copy in loads[:4]:
        copy.wait()
    parent = keep_rows(kids, counts)
    terms = lax.dot_general(
        added[...].astype(BF16),
        apart([writes[...]], kids),
        (((0,), (0,)), ((), ())),
        preferred_element_type=F32,
    )
    for copy in loads[4:6]:
        copy.wait()
    for k in range(kids):
        for i in range(heads):
            factor = jnp.broadcast_to(
                kept[k : k + 1, i * headdim : i * headdim + 1], (headdim, state)
            )
            fin[k, i] = (
                win[parent[k], i] * factor
                + terms[i * headdim : (i + 1) * headdim, k * state : (k + 1) * state]
            )
        pltpu.make_async_copy(fin.at[k], final_state.at[k], out_sem.at[k]).start()
    loads[6].wait()
    bands, cuts = own // 16, mixed.shape[2] // LANES
    for r in range(bands):
        answer = [jnp.zeros((16, LANES), F32) for _ in range(cuts)]
        for g in range(GROUPS):
            square = jnp.zeros((16, 1), F32)
            total = [jnp.zeros((16, LANES), F32) for _ in range(cuts)]
            for s in range(g * span, (g + 1) * span):
                mark = parts[s, bands * cuts].astype(F32)[:, 2 * r : 2 * r + 2]
                square = square + mark[:, 0:1] + mark[:, 1:2]
                for i in range(cuts):
                    total[i] = total[i] + parts[s, r * cuts + i].astype(F32)
            scale = lax.rsqrt(square / (width * span) + EPSILON)
            answer = [a + b * scale for a, b in zip(answer, total)]
        answer = jnp.concatenate(answer, axis=1)
        each = 16 // steps
        for k in range(each):
            mixed[r * each + k] = answer[k * steps : (k + 1) * steps].astype(BF16)
    loads[7].wait()
    for k in range(kids):
        pltpu.make_async_copy(fin.at[k], final_state.at[k], out_sem.at[k]).wait()


def on_device(
    np_,
    nh,
    counts,
    ssm_state,
    conv_value,
    conv_wread,
    token_ids,
    embedding,
    w_gate,
    w_value,
    w_wread,
    w_step,
    kern_value,
    bias_value,
    kern_wread,
    bias_wread,
    step_bias,
    decay_log,
    skip_gain,
    norm_gain,
    w_output,
):
    kids, heads, headdim, state = ssm_state.shape
    steps = token_ids.shape[1]
    own = kids * steps
    rows = np_ * own
    owned = rows // 2 // nh
    depth, width = w_value.shape
    cols = w_output.shape[1]
    zs = np_ // 2
    span = nh // GROUPS
    taps = kern_value.shape[0]
    tiles = own // 16 * (width // LANES) + 1
    dma = pltpu.SemaphoreType.DMA
    smem = pltpu.SMEM
    vmem = pltpu.VMEM
    scratch = [
        smem((kids,), jnp.int32),
        smem((heads,), F32),
        smem((heads,), F32),
        smem((heads,), F32),
        vmem((steps, np_ * kids), jnp.int32),
        vmem((np_ * kids, 8), jnp.int32),
        vmem((taps, width), F32),
        vmem((1, width), F32),
        vmem((1, 2 * state), F32),
        vmem((1, width), F32),
        vmem(embedding.shape, BF16),
        vmem((depth, width), BF16),
        vmem((depth, width), BF16),
        vmem((depth, state), BF16),
        vmem((heads, depth), BF16),
        vmem((width, cols), BF16),
        vmem((kids, heads, headdim, state), F32),
        vmem((2, 3, kids, width), F32),
        vmem((2, 3, kids, 2 * state), F32),
        vmem((taps, 2 * state), F32),
        vmem((width, kids * state), BF16),
        vmem((3, kids, width), F32),
        vmem((3, kids, 2 * state), F32),
        vmem((2, nh, owned, depth), BF16),
        vmem((2, nh - 1, owned, depth), BF16),
        vmem((2, nh, owned, depth), BF16),
        vmem((2, zs, own, LANES), BF16),
        vmem((2, zs, own, width), BF16),
        vmem((2, zs, own, width), BF16),
        vmem((zs, own, LANES), BF16),
        vmem((zs, own, width), BF16),
        vmem((zs, own, width), BF16),
        vmem((zs - 1, own, LANES), BF16),
        vmem((zs - 1, own, width), BF16),
        vmem((zs - 1, own, width), BF16),
        vmem((zs - 1, own, LANES), BF16),
        vmem((zs - 1, own, width), BF16),
        vmem((zs - 1, own, width), BF16),
        vmem((span, own, LANES), BF16),
        vmem((np_, tiles, 16, LANES), BF16),
        vmem((zs, 2, tiles, 16, LANES), BF16),
        vmem((kids, width), F32),
        vmem((own, width), F32),
        vmem((own, state), F32),
        vmem((3, kids, width), F32),
        dma,
        dma((EMB_PIECES,)),
        dma((20,)),
        dma((4,)),
        dma((4,)),
        dma((2, nh - 1)),
        dma((2, nh - 1)),
        dma((2, nh - 1)),
        dma((2, nh - 1)),
        dma((3, 2)),
        dma((3, 2)),
        dma((3, zs - 1)),
        dma((3, zs - 1)),
        dma((span - 1,)),
        dma((span - 1,)),
        dma((zs - 1,)),
        dma((zs - 1,)),
        dma((zs,)),
        dma((zs,)),
        dma((zs, 2)),
        dma((nh,)),
        dma,
        dma((5,)),
    ]
    hbm = pl.BlockSpec(memory_space=pltpu.HBM)
    limit = 60 * 1024 * 1024
    shape = jax.ShapeDtypeStruct
    parts, below, kept, added, writes, conv = pl.pallas_call(
        functools.partial(fused, np_, nh),
        out_shape=(
            shape((nh, tiles, 16, LANES), BF16),
            shape((heads, headdim, state), F32),
            shape((kids, width), F32),
            shape((own, width), F32),
            shape((own, state), F32),
            shape((3, kids, width), F32),
        ),
        in_specs=[hbm] * 19,
        out_specs=(hbm,) * 6,
        scratch_shapes=scratch,
        compiler_params=pltpu.CompilerParams(
            collective_id=0, has_side_effects=True, vmem_limit_bytes=limit
        ),
    )(
        counts,
        step_bias,
        decay_log,
        skip_gain,
        token_ids.T,
        kern_value,
        bias_value.reshape(1, -1),
        kern_wread,
        bias_wread.reshape(1, -1),
        norm_gain.reshape(1, -1),
        ssm_state,
        conv_value.transpose(1, 0, 2),
        conv_wread.transpose(1, 0, 2),
        embedding,
        w_gate,
        w_value,
        w_wread,
        w_step.T,
        w_output,
    )
    mixed, final_state, final_conv = pl.pallas_call(
        functools.partial(finish, nh),
        out_shape=(
            shape((kids, steps, cols), BF16),
            shape(ssm_state.shape, F32),
            shape((3, kids, width), F32),
        ),
        in_specs=[hbm] * 8,
        out_specs=(pl.BlockSpec(memory_space=pltpu.VMEM), hbm, hbm),
        scratch_shapes=[
            vmem((nh, tiles, 16, LANES), BF16),
            vmem((kids, width), F32),
            vmem((own, width), F32),
            vmem((own, state), F32),
            smem((kids,), jnp.int32),
            vmem((kids, heads, headdim, state), F32),
            vmem((kids, heads, headdim, state), F32),
            dma((8,)),
            dma,
            dma((kids,)),
        ],
        compiler_params=pltpu.CompilerParams(vmem_limit_bytes=limit),
    )(parts, below, kept, added, writes, conv, counts, ssm_state)
    return mixed, final_state, final_conv.transpose(1, 0, 2)


def solution(mesh):
    return jax.shard_map(
        functools.partial(on_device, mesh.shape["particle"], mesh.shape["head"]),
        mesh=mesh,
        in_specs=(
            P("particle"),
            P("particle", "head", None, None),
            P("particle", None, "head"),
            P("particle", None, None),
            P(),
            P("head", "particle"),
            P("particle", "head"),
            P("particle", "head"),
            P("particle", None),
            P("particle", "head"),
            P(None, "head"),
            P("head"),
            P(),
            P(),
            P("head"),
            P("head"),
            P("head"),
            P("head"),
            P("head", "particle"),
        ),
        out_specs=(
            P("head", None, "particle"),
            P("particle", "head", None, None),
            P("particle", None, "head"),
        ),
        check_vma=False,
    )
```

```python
import functools

import jax
import jax.numpy as jnp
from jax import lax
from jax.experimental import pallas as pl
from jax.experimental.pallas import tpu as pltpu
from jax.sharding import PartitionSpec as P

GROUPS = 4
EPSILON = 1e-05
MESH = pl.DeviceIdType.MESH
F32 = jnp.float32
BF16 = jnp.bfloat16
LANES = 128
EMB_PIECES = 4


def silu(x):
    return x * (1.0 / (1.0 + jnp.exp(-x)))


def softplus(x):
    return jnp.maximum(x, 0.0) + jnp.log1p(jnp.exp(-jnp.abs(x)))


def iota(shape, axis):
    return lax.broadcasted_iota(jnp.int32, shape, axis)


def keep_rows(kids, counts):
    counted = counts[0]
    for i in range(1, kids - 1):
        counted = counted + counts[i]
    running = kids - counted
    marks = [running]
    for i in range(kids - 1):
        running = running + counts[i]
        marks.append(running)
    parent = []
    for k in range(kids):
        at = jnp.int32(0)
        for mark in marks:
            at = at + (mark <= k).astype(jnp.int32)
        parent.append(jnp.minimum(at, kids - 1))
    return parent


def apart(blocks, kids):
    whole = jnp.concatenate(blocks, axis=0)
    child = iota(whole.shape, 0) % kids
    return jnp.concatenate(
        [jnp.where(child == k, whole, 0.0) for k in range(kids)], axis=1
    ).astype(BF16)


def fused(
    np_,
    nh,
    counts_h,
    step_bias_h,
    decay_log_h,
    skip_gain_h,
    tok_h,
    kern_value_h,
    bias_value_h,
    kern_wread,
    bias_wread,
    norm_gain_h,
    ssm,
    conv_value,
    conv_wread,
    emb,
    w_gate,
    w_value,
    w_wread,
    w_step,
    w_output,
    parts_o,
    states_o,
    conv_o,
    counts,
    step_bias,
    decay_log,
    skip_gain,
    tok,
    ids_s,
    kern_value,
    bias_value,
    bw_v,
    norm_gain,
    emb_v,
    wg_v,
    wv_v,
    ww_v,
    ws_v,
    wo_v,
    win,
    cwin,
    wwin,
    kw_v,
    sbf,
    hist,
    whist,
    tok_part,
    tok_recv,
    tok_all,
    term_w,
    term_v,
    term_g,
    sib_w,
    sib_v,
    sib_g,
    out_w,
    out_v,
    out_far,
    out_near,
    in_w,
    in_v,
    in_far,
    in_near,
    quarter,
    nrm_all,
    part,
    fin,
    conv_v,
    tok_sem,
    emb_sem,
    loc_sem,
    shift_send,
    shift_recv,
    rs_send,
    rs_recv,
    ag_send,
    ag_recv,
    sib_send,
    sib_recv,
    z_send,
    z_recv,
    far_send,
    far_recv,
    near_send,
    near_recv,
    mate_send,
    mate_recv,
    nrm_send,
    nrm_recv,
    fwd_send,
    fwd_recv,
    out_send,
    out_recv,
    own_sem,
    res_sem,
):
    p = lax.axis_index("particle")
    h = lax.axis_index("head")
    zs = np_ // 2
    z = p // 2
    c = p % 2
    sibling = z * 2 + 1 - c
    kids = counts.shape[0]
    steps = tok.shape[0]
    own = kids * steps
    rows = np_ * own
    width = wv_v.shape[1]
    state = ssm.shape[3]
    heads = ssm.shape[1]
    headdim = ssm.shape[2]
    vocab = emb.shape[0]
    span = nh // GROUPS
    group, mate = h // span, h % span
    share = 2 * state // span
    half = rows // 2
    owned = half // nh
    reach = zs // 2
    order = [reach]
    for d in range(reach - 1, 0, -1):
        order += [d, -d]
    order.append(0)

    def chip(d):
        return lax.rem(z + d + zs, zs)

    barrier = pltpu.get_barrier_semaphore()

    def greet_head(j, _):
        pl.semaphore_signal(
            barrier, inc=1, device_id={"head": lax.rem(h + j, nh)}, device_id_type=MESH
        )
        return 0

    def greet_particle(j, _):
        pl.semaphore_signal(
            barrier, inc=1, device_id={"particle": lax.rem(p + j, np_)}, device_id_type=MESH
        )
        return 0

    lax.fori_loop(1, nh, greet_head, 0)
    lax.fori_loop(1, np_, greet_particle, 0)

    tok_copy = pltpu.make_async_copy(tok_h, tok, tok_sem)
    tok_copy.start()
    piece = vocab // EMB_PIECES
    emb_copies = [
        pltpu.make_async_copy(
            emb.at[pl.ds(i * piece, piece)], emb_v.at[pl.ds(i * piece, piece)], emb_sem.at[i]
        )
        for i in range(EMB_PIECES)
    ]
    for copy in emb_copies:
        copy.start()
    at_write = pl.ds(pl.multiple_of(group * state, state), state)
    at_read = pl.ds(pl.multiple_of((GROUPS + group) * state, state), state)
    side = mate // (span // 2)
    at_share = pl.ds(pl.multiple_of((side * GROUPS + group) * state, state), state)
    lo, hi = pl.ds(0, state), pl.ds(state, state)
    pairs = [
        (ssm.at[pl.ds(0, kids - 1)], win.at[pl.ds(1, kids - 1)]),
        (conv_value, cwin.at[1]),
        (conv_wread.at[:, :, at_write], wwin.at[1, :, :, lo]),
        (conv_wread.at[:, :, at_read], wwin.at[1, :, :, hi]),
        (counts_h, counts),
        (w_wread.at[:, at_share], ww_v),
        (w_step, ws_v),
        (w_value, wv_v),
        (w_gate, wg_v),
        (kern_wread.at[:, at_write], kw_v.at[:, lo]),
        (kern_wread.at[:, at_read], kw_v.at[:, hi]),
        (w_output, wo_v),
        (step_bias_h, step_bias),
        (decay_log_h, decay_log),
        (skip_gain_h, skip_gain),
        (kern_value_h, kern_value),
        (bias_value_h, bias_value),
        (norm_gain_h, norm_gain),
        (bias_wread.at[:, at_write], bw_v.at[:, lo]),
        (bias_wread.at[:, at_read], bw_v.at[:, hi]),
    ]
    loads = [pltpu.make_async_copy(s, d, loc_sem.at[i]) for i, (s, d) in enumerate(pairs)]
    for copy in loads:
        copy.start()

    tok_copy.wait()
    ids_t = jnp.concatenate([tok[...], jnp.zeros((8 - steps, np_ * kids), jnp.int32)], axis=0).T
    ids_s[...] = ids_t - h * vocab

    def lookup(m):
        column = []
        for d in order[m * reach : (m + 1) * reach]:
            pair = ids_s[pl.ds(pl.multiple_of(chip(d) * 2 * kids, 2 * kids), 2 * kids), :]
            for core in range(2):
                for t in range(steps):
                    column.append(pair[core * kids : (core + 1) * kids, t : t + 1])
        ids = jnp.concatenate(column, axis=0)
        total = None
        for i in range(EMB_PIECES):
            if m == 0:
                emb_copies[i].wait()
            hot = jnp.where(ids - i * piece == iota((half, piece), 1), 1.0, 0.0).astype(BF16)
            term = jnp.dot(hot, emb_v[pl.ds(i * piece, piece)], preferred_element_type=F32)
            total = term if total is None else total + term
        tok_part[m] = total.astype(BF16).reshape(nh, owned, -1)

    def rs_copy(m, j):
        dest = lax.rem(h + j, nh)
        return pltpu.make_async_remote_copy(
            src_ref=tok_part.at[m, dest],
            dst_ref=tok_recv.at[m, j - 1],
            send_sem=rs_send.at[m, j - 1],
            recv_sem=rs_recv.at[m, j - 1],
            device_id={"head": dest},
            device_id_type=MESH,
        )

    def ag_copy(m, j):
        return pltpu.make_async_remote_copy(
            src_ref=tok_all.at[m, h],
            dst_ref=tok_all.at[m, h],
            send_sem=ag_send.at[m, j - 1],
            recv_sem=ag_recv.at[m, j - 1],
            device_id={"head": lax.rem(h + j, nh)},
            device_id_type=MESH,
        )

    def ag_back(m, j):
        source = lax.rem(h + nh - j, nh)
        return pltpu.make_async_remote_copy(
            src_ref=tok_all.at[m, h],
            dst_ref=tok_all.at[m, source],
            send_sem=ag_send.at[m, j - 1],
            recv_sem=ag_recv.at[m, j - 1],
            device_id={"head": source},
            device_id_type=MESH,
        )

    def each(do):
        def step(j, _):
            do(j)
            return 0

        lax.fori_loop(1, nh, step, 0)

    lookup(0)
    pl.semaphore_wait(barrier, nh - 1 + np_ - 1)
    each(lambda j: rs_copy(0, j).start())

    above = lax.rem(p + 1, np_)
    shift_pairs = [
        (ssm.at[kids - 1], win.at[0]),
        (conv_value, cwin.at[0]),
        (conv_wread.at[:, :, at_write], wwin.at[0, :, :, lo]),
        (conv_wread.at[:, :, at_read], wwin.at[0, :, :, hi]),
    ]
    shifts = [
        pltpu.make_async_remote_copy(
            src_ref=s,
            dst_ref=d,
            send_sem=shift_send.at[i],
            recv_sem=shift_recv.at[i],
            device_id={"particle": above},
            device_id_type=MESH,
        )
        for i, (s, d) in enumerate(shift_pairs)
    ]
    for copy in shifts:
        copy.start()
    lookup(1)
    each(lambda j: rs_copy(1, j).start())

    for m in range(2):
        each(lambda j, m=m: rs_copy(m, j).wait_recv())
        shared = tok_part[m, h]
        for s in range(nh - 1):
            shared = shared + tok_recv[m, s]
        tok_all[m, h] = shared
        each(lambda j, m=m: ag_copy(m, j).start())

    for copy in loads[:5]:
        copy.wait()
    parent = keep_rows(kids, counts)
    for copy in shifts:
        copy.wait_recv()
    for k in range(kids):
        sbf[:, pl.ds(k * state, state)] = win[parent[k]].reshape(width, state).astype(BF16)
        here = jnp.minimum(parent[k], 1)
        row = pl.ds(jnp.where(parent[k] == 0, kids - 1, parent[k] - 1), 1)
        for tap in range(3):
            hist[tap, pl.ds(k, 1), :] = cwin[here, tap, row, :]
            whist[tap, pl.ds(k, 1), :] = wwin[here, tap, row, :]
    for copy in loads[5:]:
        copy.wait()

    kinds = [
        (term_w, sib_w, out_w, in_w),
        (term_v, sib_v, out_v, in_v),
        (term_g, sib_g),
    ]

    def sib_copy(kind, m):
        source, target = kinds[kind][:2]
        return pltpu.make_async_remote_copy(
            src_ref=source.at[1 - c, pl.ds(m * reach, reach)],
            dst_ref=target.at[pl.ds(m * reach, reach)],
            send_sem=sib_send.at[kind, m],
            recv_sem=sib_recv.at[kind, m],
            device_id={"particle": sibling},
            device_id_type=MESH,
        )

    def along(d):
        return {"particle": lax.rem(p + 2 * d + np_, np_)}

    def z_copy(kind, i):
        _, _, out, back = kinds[kind]
        return pltpu.make_async_remote_copy(
            src_ref=out.at[i],
            dst_ref=back.at[i],
            send_sem=z_send.at[kind, i],
            recv_sem=z_recv.at[kind, i],
            device_id=along(order[i]),
            device_id_type=MESH,
        )

    def place(kind, m, terms):
        source = kinds[kind][0]
        for b in range(2 * reach):
            block = terms[b * own : (b + 1) * own].astype(BF16)
            source[b % 2, m * reach + b // 2] = block.reshape(source.shape[2:])
        sib_copy(kind, m).start()

    def chip_sum(kind, i):
        return kinds[kind][0][c, i].astype(F32) + kinds[kind][1][i].astype(F32)

    def send_sums(kind, which):
        for i in which:
            kinds[kind][2][i] = chip_sum(kind, i).astype(BF16)
            z_copy(kind, i).start()

    def arrive(kind):
        total = chip_sum(kind, zs - 1)
        for i in range(zs - 1):
            z_copy(kind, i).wait_recv()
            total = total + kinds[kind][3][i].astype(F32)
        return total.astype(BF16)

    def gate_sum(d, q):
        i = order.index(d)
        return term_g[c, i, q].astype(F32) + sib_g[i, q].astype(F32)

    def whole(q, way):
        return (way == 1) == (q == 0)

    def far_copy(q, way):
        side = (1 - way) // 2
        cut = pl.ds(0, 2) if whole(q, way) else pl.ds(1, 1)
        return pltpu.make_async_remote_copy(
            src_ref=out_far.at[q, side, cut],
            dst_ref=in_far.at[q, side, cut],
            send_sem=far_send.at[q, side],
            recv_sem=far_recv.at[q, side],
            device_id=along(2 * way),
            device_id_type=MESH,
        )

    def near_copy(q, way, n):
        side = (1 - way) // 2
        return pltpu.make_async_remote_copy(
            src_ref=out_near.at[q, side, n],
            dst_ref=in_near.at[q, side, n],
            send_sem=near_send.at[q, side, n],
            recv_sem=near_recv.at[q, side, n],
            device_id=along((2 - n) * way),
            device_id_type=MESH,
        )

    legs = [(q, way) for q in range(2) for way in (1, -1)]

    for m in range(2):
        each(lambda j, m=m: ag_back(m, j).wait_recv())
        tokens = tok_all[m].reshape(half, -1)
        matrices = jnp.dot(tokens, ww_v[...], preferred_element_type=F32)
        rate = lax.dot_general(
            tokens, ws_v[...], (((1,), (1,)), ((), ())), preferred_element_type=F32
        )
        pads = [jnp.zeros((half, n), F32) for n in (share, LANES - share - heads)]
        rate = jnp.concatenate([pads[0], rate, pads[1]], axis=1)
        turned = jnp.concatenate([matrices[:, share:], matrices[:, :share]], axis=1)
        matrices = jnp.where(mate % (span // 2) == 0, matrices, turned)
        place(0, m, jnp.where(iota((half, LANES), 1) < share, matrices, rate))
        place(2, m, jnp.dot(tokens, wg_v[...], preferred_element_type=F32))
        place(1, m, jnp.dot(tokens, wv_v[...], preferred_element_type=F32))
        sib_copy(0, m).wait_recv()
        send_sums(0, range(m * reach, min((m + 1) * reach, zs - 1)))
        sib_copy(2, m).wait_recv()
        if m == 0:
            for q, way in legs:
                side = (1 - way) // 2
                if whole(q, way):
                    out_far[q, side, 0] = gate_sum(reach, q).astype(BF16)
                out_far[q, side, 1] = gate_sum(way * (reach - 1), q).astype(BF16)
                far_copy(q, way).start()
        sib_copy(1, m).wait_recv()
        send_sums(1, range(1) if m == 0 else range(1, zs - 1))
    for q, way in legs:
        side = (1 - way) // 2
        far_copy(q, way).wait_recv()
        for n in range(2):
            term = gate_sum(way * (2 - n), q)
            if n == 1 or whole(q, way):
                term = term + in_far[q, side, n].astype(F32)
            out_near[q, side, n] = term.astype(BF16)
            near_copy(q, way, n).start()

    def arrive_gate(q):
        total = gate_sum(0, q)
        for side, way in enumerate((1, -1)):
            for n in range(2):
                near_copy(q, way, n).wait_recv()
                total = total + in_near[q, side, n].astype(F32)
        return total.astype(BF16)

    narrow = arrive(0)
    quarter[mate] = narrow

    def mate_copy(j):
        return pltpu.make_async_remote_copy(
            src_ref=quarter.at[mate],
            dst_ref=quarter.at[mate],
            send_sem=mate_send.at[j - 1],
            recv_sem=mate_recv.at[j - 1],
            device_id={"head": group * span + lax.rem(mate + j, span)},
            device_id_type=MESH,
        )

    def mate_back(j):
        source = lax.rem(mate + span - j, span)
        return pltpu.make_async_remote_copy(
            src_ref=quarter.at[mate],
            dst_ref=quarter.at[source],
            send_sem=mate_send.at[j - 1],
            recv_sem=mate_recv.at[j - 1],
            device_id={"head": group * span + source},
            device_id_type=MESH,
        )

    for j in range(1, span):
        mate_copy(j).start()

    def at_step(a, t):
        return a[t * kids : (t + 1) * kids]

    spread = (
        iota((LANES, width), 1) // headdim + share == iota((LANES, width), 0)
    ).astype(F32)
    rates = jnp.dot(narrow, spread.astype(BF16), preferred_element_type=F32)
    lane_head = iota((1, width), 1) // headdim

    def per_head(ref):
        out = jnp.zeros((1, width), F32)
        for i in range(heads):
            out = jnp.where(lane_head == i, ref[i], out)
        return out

    step_size = softplus(rates + per_head(step_bias))
    decay = jnp.exp(-step_size * jnp.exp(per_head(decay_log)))
    skip = per_head(skip_gain)

    def convolve(past, current, kern, bias):
        seq = [past[i] for i in range(3)] + [at_step(current, t) for t in range(steps)]
        out = []
        for t in range(steps):
            a = seq[t] * kern[0:1]
            for i in range(1, 4):
                a = a + seq[t + i] * kern[i : i + 1]
            out.append(silu(a + bias))
        return out

    for j in range(1, span):
        mate_back(j).wait_recv()
    wread = jnp.concatenate([quarter[i].astype(F32)[:, :share] for i in range(span)], axis=1)
    conv_w = convolve(whist, wread, kw_v[...], bw_v[...])
    writes = [a[:, :state] for a in conv_w]
    reads = [a[:, state:] for a in conv_w]
    first = lax.dot_general(
        apart(reads, kids), sbf[...], (((1,), (1,)), ((), ())), preferred_element_type=F32
    )
    value = arrive(1).astype(F32)
    conv = convolve(hist, value, kern_value[...], bias_value[...])

    kept = None
    added = []
    readings = []
    for t in range(steps):
        now = at_step(decay, t)
        kept = now if kept is None else kept * now
        added = [a * now for a in added] + [at_step(step_size, t) * conv[t]]
        reading = kept * at_step(first, t) + skip * conv[t]
        for u in range(t + 1):
            match = jnp.sum(writes[u] * reads[t], axis=1, keepdims=True)
            reading = reading + added[u] * match
        readings.append(reading)
    gate = jnp.concatenate([arrive_gate(q) for q in range(2)], axis=0).astype(F32)
    gated = jnp.concatenate(readings, axis=0) * silu(gate)

    squares = jnp.sum(gated * gated, axis=1, keepdims=True)
    upper = squares.astype(BF16).astype(F32)
    lane = iota((own, LANES), 1)
    squares = jnp.where(lane % 2 == 0, upper, squares - upper).astype(BF16)
    scaled = jnp.concatenate([(gated * norm_gain[...]).astype(BF16), squares], axis=1)
    at_row, from_row = iota((own, own), 0), iota((own, own), 1)
    turn = (from_row == (at_row % steps) * kids + at_row // steps).astype(F32).astype(BF16)
    scaled = jnp.dot(turn, scaled, preferred_element_type=F32)
    bands, cuts = own // 16, width // LANES
    marks = scaled[:16, width:]
    for r in range(bands):
        band = scaled[r * 16 : (r + 1) * 16]
        for i in range(cuts):
            nrm_all[p, r * cuts + i] = band[:, i * LANES : (i + 1) * LANES].astype(BF16)
        if r > 0:
            marks = jnp.where(iota(marks.shape, 1) < 2 * r, marks, band[:, width:])
    nrm_all[p, bands * cuts] = marks.astype(BF16)

    def nrm_copy(at, target, send, recv):
        return pltpu.make_async_remote_copy(
            src_ref=nrm_all.at[at],
            dst_ref=nrm_all.at[at],
            send_sem=send,
            recv_sem=recv,
            device_id={"particle": target},
            device_id_type=MESH,
        )

    def direct(i):
        target = lax.rem(p + 2 * order[i] + np_, np_)
        return nrm_copy(p, target, nrm_send.at[i], nrm_recv.at[i])

    def forward(i):
        at = lax.rem(p - 2 * order[i] + np_, np_)
        return nrm_copy(at, sibling, fwd_send.at[i], fwd_recv.at[i])

    for i in reversed(range(zs - 1)):
        direct(i).start()
    forward(zs - 1).start()

    adds = lax.dot_general(
        jnp.concatenate(added, axis=0).astype(BF16),
        apart(writes, kids),
        (((0,), (0,)), ((), ())),
        preferred_element_type=F32,
    )
    for k in range(kids):
        for i in range(heads):
            factor = jnp.broadcast_to(
                kept[k : k + 1, i * headdim : i * headdim + 1], (headdim, state)
            )
            fin[k, i] = (
                win[parent[k], i] * factor
                + adds[i * headdim : (i + 1) * headdim, k * state : (k + 1) * state]
            )
    for i in range(3):
        conv_v[i] = at_step(value, steps - 3 + i)
    results = [
        pltpu.make_async_copy(s, d, res_sem.at[i])
        for i, (s, d) in enumerate([(fin, states_o), (conv_v, conv_o)])
    ]
    for copy in results:
        copy.start()

    def dest_of(i, core):
        return lax.rem(z - order[i] + zs, zs) * 2 + core

    def out_copy(i, core):
        return pltpu.make_async_remote_copy(
            src_ref=part.at[i, core],
            dst_ref=parts_o.at[h],
            send_sem=out_send.at[i, core],
            recv_sem=out_recv.at[h],
            device_id={"head": dest_of(i, core)},
            device_id_type=MESH,
        )

    def own_copy(i, core):
        return pltpu.make_async_copy(part.at[i, core], parts_o.at[h], own_sem)

    def send_parts(places):
        block = []
        for i in places:
            for core in range(2):
                tiles = nrm_all[dest_of(i, core)]
                for r in range(bands):
                    block.append(
                        jnp.concatenate([tiles[r * cuts + n] for n in range(cuts)], axis=1)
                    )
        product = jnp.dot(
            jnp.concatenate(block, axis=0), wo_v[...], preferred_element_type=F32
        ).astype(BF16)
        for n, i in enumerate(places):
            for core in range(2):
                for r in range(bands):
                    start = (2 * n + core) * own + r * 16
                    for e in range(cuts):
                        part[i, core, r * cuts + e] = product[
                            start : start + 16, e * LANES : (e + 1) * LANES
                        ]
                part[i, core, bands * cuts] = nrm_all[dest_of(i, core), bands * cuts]
        for i in places:
            for core in range(2):
                dest = dest_of(i, core)

                @pl.when(dest != h)
                def _(i=i, core=core):
                    out_copy(i, core).start()

                @pl.when(dest == h)
                def _(i=i, core=core):
                    own_copy(i, core).start()

    def take(i):
        at = lax.rem(p - 2 * order[i] + np_, np_)
        if order[i] != 0:
            nrm_copy(at, sibling, nrm_send.at[i], nrm_recv.at[i]).wait_recv()
            forward(i).start()

    def take_forward(i):
        at = lax.rem(sibling - 2 * order[i] + np_, np_)
        nrm_copy(at, sibling, fwd_send.at[i], fwd_recv.at[i]).wait_recv()

    near = list(range(zs))[::-1]
    batches = [near[:3], near[3:5], near[5:]]
    for batch in batches:
        for i in batch:
            take(i)
        for i in batch:
            take_forward(i)
        send_parts(batch)

    for m in range(2):
        each(lambda j, m=m: rs_copy(m, j).wait_send())
        each(lambda j, m=m: ag_copy(m, j).wait_send())
    for copy in shifts:
        copy.wait_send()
    for kind in range(3):
        for m in range(2):
            sib_copy(kind, m).wait_send()
    for kind in range(2):
        for i in range(zs - 1):
            z_copy(kind, i).wait_send()
    for q, way in legs:
        far_copy(q, way).wait_send()
        for n in range(2):
            near_copy(q, way, n).wait_send()
    for j in range(1, span):
        mate_copy(j).wait_send()
    for i in range(zs - 1):
        direct(i).wait_send()
    for i in range(zs):
        forward(i).wait_send()
    for copy in results:
        copy.wait()
    for i in range(zs):
        for core in range(2):
            dest = dest_of(i, core)

            @pl.when(dest != h)
            def _(i=i, core=core):
                out_copy(i, core).wait_send()

    own_copy(0, 0).wait()

    def out_wait(s, _):
        @pl.when(s != h)
        def _():
            pltpu.make_async_remote_copy(
                src_ref=part.at[0, 0],
                dst_ref=parts_o.at[s],
                send_sem=out_send.at[0, 0],
                recv_sem=out_recv.at[s],
                device_id={"head": s},
                device_id_type=MESH,
            ).wait_recv()

        return 0

    lax.fori_loop(0, nh, out_wait, 0)


def finish(
    nh,
    steps,
    parts_h,
    states_h,
    conv_h,
    mixed,
    final_state,
    final_conv,
    parts,
    states,
    conv,
    in_sems,
    out_sems,
):
    kids, heads, headdim, _ = states_h.shape
    width = heads * headdim
    span = nh // GROUPS
    load = pltpu.make_async_copy(parts_h, parts, in_sems.at[kids + 1])
    pairs = [(states_h.at[k], states.at[k], final_state.at[k]) for k in range(kids)]
    pairs.append((conv_h, conv, final_conv))
    pulls = [pltpu.make_async_copy(a, b, in_sems.at[i]) for i, (a, b, _) in enumerate(pairs)]
    pushes = [pltpu.make_async_copy(b, d, out_sems.at[i]) for i, (_, b, d) in enumerate(pairs)]
    for copy in pulls:
        copy.start()
    load.start()
    for pull, push in zip(pulls, pushes):
        pull.wait()
        push.start()
    load.wait()
    cuts = mixed.shape[2] // LANES
    bands = (parts.shape[1] - 1) // cuts
    for r in range(bands):
        answer = [jnp.zeros((16, LANES), F32) for _ in range(cuts)]
        for g in range(GROUPS):
            square = jnp.zeros((16, 1), F32)
            total = [jnp.zeros((16, LANES), F32) for _ in range(cuts)]
            for s in range(g * span, (g + 1) * span):
                mark = parts[s, bands * cuts].astype(F32)[:, 2 * r : 2 * r + 2]
                square = square + mark[:, 0:1] + mark[:, 1:2]
                for i in range(cuts):
                    total[i] = total[i] + parts[s, r * cuts + i].astype(F32)
            scale = lax.rsqrt(square / (width * span) + EPSILON)
            answer = [a + b * scale for a, b in zip(answer, total)]
        answer = jnp.concatenate(answer, axis=1)
        each = 16 // steps
        for k in range(each):
            mixed[r * each + k] = answer[k * steps : (k + 1) * steps].astype(BF16)
    for copy in pushes:
        copy.wait()


def on_device(
    np_,
    nh,
    counts,
    ssm_state,
    conv_value,
    conv_wread,
    token_ids,
    embedding,
    w_gate,
    w_value,
    w_wread,
    w_step,
    kern_value,
    bias_value,
    kern_wread,
    bias_wread,
    step_bias,
    decay_log,
    skip_gain,
    norm_gain,
    w_output,
):
    kids, heads, headdim, state = ssm_state.shape
    steps = token_ids.shape[1]
    own = kids * steps
    rows = np_ * own
    owned = rows // 2 // nh
    depth, width = w_value.shape
    cols = w_output.shape[1]
    zs = np_ // 2
    span = nh // GROUPS
    taps = kern_value.shape[0]
    tiles = own // 16 * (width // LANES) + 1
    dma = pltpu.SemaphoreType.DMA
    smem = pltpu.SMEM
    vmem = pltpu.VMEM
    scratch = [
        smem((kids,), jnp.int32),
        smem((heads,), F32),
        smem((heads,), F32),
        smem((heads,), F32),
        vmem((steps, np_ * kids), jnp.int32),
        vmem((np_ * kids, 8), jnp.int32),
        vmem((taps, width), F32),
        vmem((1, width), F32),
        vmem((1, 2 * state), F32),
        vmem((1, width), F32),
        vmem(embedding.shape, BF16),
        vmem((depth, width), BF16),
        vmem((depth, width), BF16),
        vmem((depth, state), BF16),
        vmem((heads, depth), BF16),
        vmem((width, cols), BF16),
        vmem((kids, heads, headdim, state), F32),
        vmem((2, 3, kids, width), F32),
        vmem((2, 3, kids, 2 * state), F32),
        vmem((taps, 2 * state), F32),
        vmem((width, kids * state), BF16),
        vmem((3, kids, width), F32),
        vmem((3, kids, 2 * state), F32),
        vmem((2, nh, owned, depth), BF16),
        vmem((2, nh - 1, owned, depth), BF16),
        vmem((2, nh, owned, depth), BF16),
        vmem((2, zs, own, LANES), BF16),
        vmem((2, zs, own, width), BF16),
        vmem((2, zs, 2, own // 2, width), BF16),
        vmem((zs, own, LANES), BF16),
        vmem((zs, own, width), BF16),
        vmem((zs, 2, own // 2, width), BF16),
        vmem((zs - 1, own, LANES), BF16),
        vmem((zs - 1, own, width), BF16),
        vmem((2, 2, 2, own // 2, width), BF16),
        vmem((2, 2, 2, own // 2, width), BF16),
        vmem((zs - 1, own, LANES), BF16),
        vmem((zs - 1, own, width), BF16),
        vmem((2, 2, 2, own // 2, width), BF16),
        vmem((2, 2, 2, own // 2, width), BF16),
        vmem((span, own, LANES), BF16),
        vmem((np_, tiles, 16, LANES), BF16),
        vmem((zs, 2, tiles, 16, LANES), BF16),
        vmem(ssm_state.shape, F32),
        vmem((3, kids, width), F32),
        dma,
        dma((EMB_PIECES,)),
        dma((20,)),
        dma((4,)),
        dma((4,)),
        dma((2, nh - 1)),
        dma((2, nh - 1)),
        dma((2, nh - 1)),
        dma((2, nh - 1)),
        dma((3, 2)),
        dma((3, 2)),
        dma((2, zs - 1)),
        dma((2, zs - 1)),
        dma((2, 2)),
        dma((2, 2)),
        dma((2, 2, 2)),
        dma((2, 2, 2)),
        dma((span - 1,)),
        dma((span - 1,)),
        dma((zs - 1,)),
        dma((zs - 1,)),
        dma((zs,)),
        dma((zs,)),
        dma((zs, 2)),
        dma((nh,)),
        dma,
        dma((2,)),
    ]
    hbm = pl.BlockSpec(memory_space=pltpu.HBM)
    limit = 60 * 1024 * 1024
    shape = jax.ShapeDtypeStruct
    parts, states, conv = pl.pallas_call(
        functools.partial(fused, np_, nh),
        out_shape=(
            shape((nh, tiles, 16, LANES), BF16),
            shape(ssm_state.shape, F32),
            shape((3, kids, width), F32),
        ),
        in_specs=[hbm] * 19,
        out_specs=(hbm,) * 3,
        scratch_shapes=scratch,
        compiler_params=pltpu.CompilerParams(
            collective_id=0, has_side_effects=True, vmem_limit_bytes=limit
        ),
    )(
        counts,
        step_bias,
        decay_log,
        skip_gain,
        token_ids.T,
        kern_value,
        bias_value.reshape(1, -1),
        kern_wread,
        bias_wread.reshape(1, -1),
        norm_gain.reshape(1, -1),
        ssm_state,
        conv_value.transpose(1, 0, 2),
        conv_wread.transpose(1, 0, 2),
        embedding,
        w_gate,
        w_value,
        w_wread,
        w_step.T,
        w_output,
    )
    mixed, final_state, final_conv = pl.pallas_call(
        functools.partial(finish, nh, steps),
        out_shape=(
            shape((kids, steps, cols), BF16),
            shape(ssm_state.shape, F32),
            shape((3, kids, width), F32),
        ),
        in_specs=[hbm] * 3,
        out_specs=(pl.BlockSpec(memory_space=pltpu.VMEM), hbm, hbm),
        scratch_shapes=[
            vmem((nh, tiles, 16, LANES), BF16),
            vmem(ssm_state.shape, F32),
            vmem((3, kids, width), F32),
            dma((kids + 2,)),
            dma((kids + 1,)),
        ],
        compiler_params=pltpu.CompilerParams(vmem_limit_bytes=limit),
    )(parts, states, conv)
    return mixed, final_state, final_conv.transpose(1, 0, 2)


def solution(mesh):
    return jax.shard_map(
        functools.partial(on_device, mesh.shape["particle"], mesh.shape["head"]),
        mesh=mesh,
        in_specs=(
            P("particle"),
            P("particle", "head", None, None),
            P("particle", None, "head"),
            P("particle", None, None),
            P(),
            P("head", "particle"),
            P("particle", "head"),
            P("particle", "head"),
            P("particle", None),
            P("particle", "head"),
            P(None, "head"),
            P("head"),
            P(),
            P(),
            P("head"),
            P("head"),
            P("head"),
            P("head"),
            P("head", "particle"),
        ),
        out_specs=(
            P("head", None, "particle"),
            P("particle", "head", None, None),
            P("particle", None, "head"),
        ),
        check_vma=False,
    )
```

```python
import functools
import math

import jax
import jax.numpy as jnp
from jax import lax
from jax.experimental import pallas as pl
from jax.experimental.pallas import tpu as pltpu
from jax.sharding import PartitionSpec as P

GROUPS = 4
EPSILON = 1e-05
MESH = pl.DeviceIdType.MESH
F32 = jnp.float32
BF16 = jnp.bfloat16
LANES = 128
EMB_PIECES = 4
BATCHES = (((0, 1, 2), 0), ((3, 4), 0), ((5, 6, 7), 1))


def silu(x):
    return x * (1.0 / (1.0 + jnp.exp(-x)))


def softplus(x):
    return jnp.maximum(x, 0.0) + jnp.log1p(jnp.exp(-jnp.abs(x)))


def iota(shape, axis):
    return lax.broadcasted_iota(jnp.int32, shape, axis)


def keep_rows(kids, counts):
    counted = counts[0]
    for i in range(1, kids - 1):
        counted = counted + counts[i]
    running = kids - counted
    marks = [running]
    for i in range(kids - 1):
        running = running + counts[i]
        marks.append(running)
    parent = []
    for k in range(kids):
        at = jnp.int32(0)
        for mark in marks:
            at = at + (mark <= k).astype(jnp.int32)
        parent.append(jnp.minimum(at, kids - 1))
    return parent


def apart(blocks, kids):
    whole = jnp.concatenate(blocks, axis=0)
    child = iota(whole.shape, 0) % kids
    return jnp.concatenate(
        [jnp.where(child == k, whole, 0.0) for k in range(kids)], axis=1
    ).astype(BF16)


def fused(
    np_,
    nh,
    counts_h,
    step_bias_h,
    decay_log_h,
    skip_gain_h,
    tok_h,
    kern_value_h,
    bias_value_h,
    kern_wread,
    bias_wread,
    norm_gain_h,
    ssm,
    conv_value,
    conv_wread,
    emb,
    w_gate,
    w_value,
    w_wread,
    w_step,
    w_output,
    mixed_o,
    states_o,
    conv_o,
    counts,
    step_bias,
    decay_log,
    skip_gain,
    tok,
    ids_s,
    kern_value,
    bias_value,
    bw_v,
    norm_gain,
    emb_v,
    wg_v,
    wv_v,
    ww_v,
    ws_v,
    wo_v,
    win,
    cwin,
    wwin,
    kw_v,
    sbf,
    hist,
    whist,
    tok_part,
    tok_recv,
    tok_all,
    term_w,
    term_v,
    term_g,
    sib_w,
    sib_v,
    sib_g,
    out_w,
    out_v,
    out_far,
    out_near,
    in_w,
    in_v,
    in_far,
    in_near,
    quarter,
    nrm_all,
    part,
    parts,
    fin,
    conv_v,
    tok_sem,
    emb_sem,
    loc_sem,
    shift_send,
    shift_recv,
    rs_send,
    rs_recv,
    ag_send,
    ag_recv,
    sib_send,
    sib_recv,
    z_send,
    z_recv,
    far_send,
    far_recv,
    near_send,
    near_recv,
    mate_send,
    mate_recv,
    nrm_send,
    nrm_recv,
    fwd_send,
    fwd_recv,
    out_send,
    out_recv,
    res_sem,
):
    p = lax.axis_index("particle")
    h = lax.axis_index("head")
    zs = np_ // 2
    z = p // 2
    c = p % 2
    sibling = z * 2 + 1 - c
    kids = counts.shape[0]
    steps = tok.shape[0]
    own = kids * steps
    rows = np_ * own
    width = wv_v.shape[1]
    state = ssm.shape[3]
    heads = ssm.shape[1]
    headdim = ssm.shape[2]
    vocab = emb.shape[0]
    span = nh // GROUPS
    group, mate = h // span, h % span
    share = 2 * state // span
    half = rows // 2
    owned = half // nh
    reach = zs // 2
    order = [reach]
    for d in range(reach - 1, 0, -1):
        order += [d, -d]
    order.append(0)

    def chip(d):
        return lax.rem(z + d + zs, zs)

    tok_copy = pltpu.make_async_copy(tok_h, tok, tok_sem)
    tok_copy.start()
    piece = vocab // EMB_PIECES
    emb_copies = [
        pltpu.make_async_copy(
            emb.at[pl.ds(i * piece, piece)], emb_v.at[pl.ds(i * piece, piece)], emb_sem.at[i]
        )
        for i in range(EMB_PIECES)
    ]
    for copy in emb_copies:
        copy.start()

    barrier = pltpu.get_barrier_semaphore()
    mates = [{"head": lax.rem(h + j, nh)} for j in range(1, nh)]
    mates += [{"particle": lax.rem(p + 2 * j, np_)} for j in range(1, zs)]
    mates += [{"particle": sibling}, {"particle": lax.rem(p + np_ - 1 + 2 * c, np_)}]
    for other in mates:
        pl.semaphore_signal(barrier, inc=1, device_id=other, device_id_type=MESH)
    at_write = pl.ds(pl.multiple_of(group * state, state), state)
    at_read = pl.ds(pl.multiple_of((GROUPS + group) * state, state), state)
    side = mate // (span // 2)
    at_share = pl.ds(pl.multiple_of((side * GROUPS + group) * state, state), state)
    lo, hi = pl.ds(0, state), pl.ds(state, state)
    pairs = [
        (ssm.at[pl.ds(0, kids - 1)], win.at[pl.ds(1, kids - 1)]),
        (conv_value, cwin.at[1]),
        (conv_wread.at[:, :, at_write], wwin.at[1, :, :, lo]),
        (conv_wread.at[:, :, at_read], wwin.at[1, :, :, hi]),
        (counts_h, counts),
        (w_wread.at[:, at_share], ww_v),
        (w_step, ws_v),
        (w_value, wv_v),
        (w_gate, wg_v),
        (kern_wread.at[:, at_write], kw_v.at[:, lo]),
        (kern_wread.at[:, at_read], kw_v.at[:, hi]),
        (w_output, wo_v),
        (step_bias_h, step_bias),
        (decay_log_h, decay_log),
        (skip_gain_h, skip_gain),
        (kern_value_h, kern_value),
        (bias_value_h, bias_value),
        (norm_gain_h, norm_gain),
        (bias_wread.at[:, at_write], bw_v.at[:, lo]),
        (bias_wread.at[:, at_read], bw_v.at[:, hi]),
    ]
    loads = [pltpu.make_async_copy(s, d, loc_sem.at[i]) for i, (s, d) in enumerate(pairs)]

    tok_copy.wait()
    ids_t = jnp.concatenate([tok[...], jnp.zeros((8 - steps, np_ * kids), jnp.int32)], axis=0).T
    ids_s[...] = ids_t - h * vocab

    def lookup(m):
        column = []
        for d in order[m * reach : (m + 1) * reach]:
            pair = ids_s[pl.ds(pl.multiple_of(chip(d) * 2 * kids, 2 * kids), 2 * kids), :]
            for core in range(2):
                for t in range(steps):
                    column.append(pair[core * kids : (core + 1) * kids, t : t + 1])
        ids = jnp.concatenate(column, axis=0)
        total = None
        for i in range(EMB_PIECES):
            if m == 0:
                emb_copies[i].wait()
            hot = jnp.where(ids - i * piece == iota((half, piece), 1), 1.0, 0.0).astype(BF16)
            term = jnp.dot(hot, emb_v[pl.ds(i * piece, piece)], preferred_element_type=F32)
            total = term if total is None else total + term
        tok_part[m] = total.astype(BF16).reshape(nh, owned, -1)

    side_x = math.isqrt(nh)
    side_y = nh // side_x
    offsets = [(a, b) for a in range(side_x) for b in range(side_y) if a or b]
    offsets.sort(key=lambda o: -min(o[0], side_x - o[0]) - min(o[1], side_y - o[1]))

    def at_offset(j, way):
        a, b = offsets[j - 1]
        x = lax.rem(h // side_y + way * a + side_x, side_x)
        y = lax.rem(h % side_y + way * b + side_y, side_y)
        return x * side_y + y

    def rs_copy(m, j):
        dest = at_offset(j, 1)
        return pltpu.make_async_remote_copy(
            src_ref=tok_part.at[m, dest],
            dst_ref=tok_recv.at[m, j - 1],
            send_sem=rs_send.at[m, j - 1],
            recv_sem=rs_recv.at[m, j - 1],
            device_id={"head": dest},
            device_id_type=MESH,
        )

    def ag_copy(m, j):
        return pltpu.make_async_remote_copy(
            src_ref=tok_all.at[m, h],
            dst_ref=tok_all.at[m, h],
            send_sem=ag_send.at[m, j - 1],
            recv_sem=ag_recv.at[m, j - 1],
            device_id={"head": at_offset(j, 1)},
            device_id_type=MESH,
        )

    def ag_back(m, j):
        source = at_offset(j, -1)
        return pltpu.make_async_remote_copy(
            src_ref=tok_all.at[m, h],
            dst_ref=tok_all.at[m, source],
            send_sem=ag_send.at[m, j - 1],
            recv_sem=ag_recv.at[m, j - 1],
            device_id={"head": source},
            device_id_type=MESH,
        )

    def each(do):
        for j in range(1, nh):
            do(j)

    lookup(0)
    pl.semaphore_wait(barrier, len(mates))
    each(lambda j: rs_copy(0, j).start())
    lookup(1)
    each(lambda j: rs_copy(1, j).start())
    for copy in loads:
        copy.start()

    above = lax.rem(p + 1, np_)
    shift_pairs = [
        (ssm.at[kids - 1], win.at[0]),
        (conv_value, cwin.at[0]),
        (conv_wread.at[:, :, at_write], wwin.at[0, :, :, lo]),
        (conv_wread.at[:, :, at_read], wwin.at[0, :, :, hi]),
    ]
    shifts = [
        pltpu.make_async_remote_copy(
            src_ref=s,
            dst_ref=d,
            send_sem=shift_send.at[i],
            recv_sem=shift_recv.at[i],
            device_id={"particle": above},
            device_id_type=MESH,
        )
        for i, (s, d) in enumerate(shift_pairs)
    ]
    for copy in shifts:
        copy.start()

    for m in range(2):
        each(lambda j, m=m: rs_copy(m, j).wait_recv())
        shared = tok_part[m, h]
        for s in range(nh - 1):
            shared = shared + tok_recv[m, s]
        tok_all[m, h] = shared
        each(lambda j, m=m: ag_copy(m, j).start())

    for copy in loads[:5]:
        copy.wait()
    parent = keep_rows(kids, counts)
    for copy in shifts:
        copy.wait_recv()
    for k in range(kids):
        sbf[:, pl.ds(k * state, state)] = win[parent[k]].reshape(width, state).astype(BF16)
        here = jnp.minimum(parent[k], 1)
        row = pl.ds(jnp.where(parent[k] == 0, kids - 1, parent[k] - 1), 1)
        for tap in range(3):
            hist[tap, pl.ds(k, 1), :] = cwin[here, tap, row, :]
            whist[tap, pl.ds(k, 1), :] = wwin[here, tap, row, :]
    for copy in loads[5:]:
        copy.wait()

    kinds = [
        (term_w, sib_w, out_w, in_w),
        (term_v, sib_v, out_v, in_v),
        (term_g, sib_g),
    ]

    def sib_copy(kind, m):
        source, target = kinds[kind][:2]
        return pltpu.make_async_remote_copy(
            src_ref=source.at[1 - c, pl.ds(m * reach, reach)],
            dst_ref=target.at[pl.ds(m * reach, reach)],
            send_sem=sib_send.at[kind, m],
            recv_sem=sib_recv.at[kind, m],
            device_id={"particle": sibling},
            device_id_type=MESH,
        )

    def along(d):
        return {"particle": lax.rem(p + 2 * d + np_, np_)}

    def z_copy(kind, i):
        _, _, out, back = kinds[kind]
        return pltpu.make_async_remote_copy(
            src_ref=out.at[i],
            dst_ref=back.at[i],
            send_sem=z_send.at[kind, i],
            recv_sem=z_recv.at[kind, i],
            device_id=along(order[i]),
            device_id_type=MESH,
        )

    def place(kind, m, terms):
        source = kinds[kind][0]
        for b in range(2 * reach):
            block = terms[b * own : (b + 1) * own].astype(BF16)
            source[b % 2, m * reach + b // 2] = block.reshape(source.shape[2:])
        sib_copy(kind, m).start()

    def chip_sum(kind, i):
        return kinds[kind][0][c, i].astype(F32) + kinds[kind][1][i].astype(F32)

    def send_sums(kind, which):
        for i in which:
            kinds[kind][2][i] = chip_sum(kind, i).astype(BF16)
            z_copy(kind, i).start()

    def arrive(kind):
        total = chip_sum(kind, zs - 1)
        for i in range(zs - 1):
            z_copy(kind, i).wait_recv()
            total = total + kinds[kind][3][i].astype(F32)
        return total.astype(BF16)

    def gate_sum(d, q):
        i = order.index(d)
        return term_g[c, i, q].astype(F32) + sib_g[i, q].astype(F32)

    def whole(q, way):
        return (way == 1) == (q == 0)

    def far_copy(q, way):
        side = (1 - way) // 2
        cut = pl.ds(0, 2) if whole(q, way) else pl.ds(1, 1)
        return pltpu.make_async_remote_copy(
            src_ref=out_far.at[q, side, cut],
            dst_ref=in_far.at[q, side, cut],
            send_sem=far_send.at[q, side],
            recv_sem=far_recv.at[q, side],
            device_id=along(2 * way),
            device_id_type=MESH,
        )

    def near_copy(q, way, n):
        side = (1 - way) // 2
        return pltpu.make_async_remote_copy(
            src_ref=out_near.at[q, side, n],
            dst_ref=in_near.at[q, side, n],
            send_sem=near_send.at[q, side, n],
            recv_sem=near_recv.at[q, side, n],
            device_id=along((2 - n) * way),
            device_id_type=MESH,
        )

    legs = [(q, way) for q in range(2) for way in (1, -1)]

    for m in range(2):
        each(lambda j, m=m: ag_back(m, j).wait_recv())
        tokens = tok_all[m].reshape(half, -1)
        matrices = jnp.dot(tokens, ww_v[...], preferred_element_type=F32)
        rate = lax.dot_general(
            tokens, ws_v[...], (((1,), (1,)), ((), ())), preferred_element_type=F32
        )
        pads = [jnp.zeros((half, n), F32) for n in (share, LANES - share - heads)]
        rate = jnp.concatenate([pads[0], rate, pads[1]], axis=1)
        turned = jnp.concatenate([matrices[:, share:], matrices[:, :share]], axis=1)
        matrices = jnp.where(mate % (span // 2) == 0, matrices, turned)
        place(0, m, jnp.where(iota((half, LANES), 1) < share, matrices, rate))
        place(2, m, jnp.dot(tokens, wg_v[...], preferred_element_type=F32))
        place(1, m, jnp.dot(tokens, wv_v[...], preferred_element_type=F32))
        sib_copy(0, m).wait_recv()
        send_sums(0, range(m * reach, min((m + 1) * reach, zs - 1)))
        sib_copy(2, m).wait_recv()
        if m == 0:
            for q, way in legs:
                side = (1 - way) // 2
                if whole(q, way):
                    out_far[q, side, 0] = gate_sum(reach, q).astype(BF16)
                out_far[q, side, 1] = gate_sum(way * (reach - 1), q).astype(BF16)
                far_copy(q, way).start()
        sib_copy(1, m).wait_recv()
        send_sums(1, range(1) if m == 0 else range(1, zs - 1))
    for q, way in legs:
        side = (1 - way) // 2
        far_copy(q, way).wait_recv()
        for n in range(2):
            term = gate_sum(way * (2 - n), q)
            if n == 1 or whole(q, way):
                term = term + in_far[q, side, n].astype(F32)
            out_near[q, side, n] = term.astype(BF16)
            near_copy(q, way, n).start()

    def arrive_gate(q):
        total = gate_sum(0, q)
        for side, way in enumerate((1, -1)):
            for n in range(2):
                near_copy(q, way, n).wait_recv()
                total = total + in_near[q, side, n].astype(F32)
        return total.astype(BF16)

    narrow = arrive(0)
    quarter[mate] = narrow

    def mate_copy(j):
        return pltpu.make_async_remote_copy(
            src_ref=quarter.at[mate],
            dst_ref=quarter.at[mate],
            send_sem=mate_send.at[j - 1],
            recv_sem=mate_recv.at[j - 1],
            device_id={"head": group * span + lax.rem(mate + j, span)},
            device_id_type=MESH,
        )

    def mate_back(j):
        source = lax.rem(mate + span - j, span)
        return pltpu.make_async_remote_copy(
            src_ref=quarter.at[mate],
            dst_ref=quarter.at[source],
            send_sem=mate_send.at[j - 1],
            recv_sem=mate_recv.at[j - 1],
            device_id={"head": group * span + source},
            device_id_type=MESH,
        )

    for j in range(1, span):
        mate_copy(j).start()

    def at_step(a, t):
        return a[t * kids : (t + 1) * kids]

    spread = (
        iota((LANES, width), 1) // headdim + share == iota((LANES, width), 0)
    ).astype(F32)
    rates = jnp.dot(narrow, spread.astype(BF16), preferred_element_type=F32)
    lane_head = iota((1, width), 1) // headdim

    def per_head(ref):
        out = jnp.zeros((1, width), F32)
        for i in range(heads):
            out = jnp.where(lane_head == i, ref[i], out)
        return out

    step_size = softplus(rates + per_head(step_bias))
    decay = jnp.exp(-step_size * jnp.exp(per_head(decay_log)))
    skip = per_head(skip_gain)

    def convolve(past, current, kern, bias):
        seq = [past[i] for i in range(3)] + [at_step(current, t) for t in range(steps)]
        out = []
        for t in range(steps):
            a = seq[t] * kern[0:1]
            for i in range(1, 4):
                a = a + seq[t + i] * kern[i : i + 1]
            out.append(silu(a + bias))
        return out

    for j in range(1, span):
        mate_back(j).wait_recv()
    wread = jnp.concatenate([quarter[i].astype(F32)[:, :share] for i in range(span)], axis=1)
    conv_w = convolve(whist, wread, kw_v[...], bw_v[...])
    writes = [a[:, :state] for a in conv_w]
    reads = [a[:, state:] for a in conv_w]
    first = lax.dot_general(
        apart(reads, kids), sbf[...], (((1,), (1,)), ((), ())), preferred_element_type=F32
    )
    kept = None
    starts = []
    for t in range(steps):
        now = at_step(decay, t)
        kept = now if kept is None else kept * now
        starts.append(kept * at_step(first, t))
    match = {
        (u, t): jnp.sum(writes[u] * reads[t], axis=1, keepdims=True)
        for t in range(steps)
        for u in range(t + 1)
    }
    value = arrive(1).astype(F32)
    conv = convolve(hist, value, kern_value[...], bias_value[...])

    added = []
    readings = []
    for t in range(steps):
        now = at_step(decay, t)
        added = [a * now for a in added] + [at_step(step_size, t) * conv[t]]
        reading = starts[t] + skip * conv[t]
        for u in range(t + 1):
            reading = reading + added[u] * match[u, t]
        readings.append(reading)
    gate = jnp.concatenate([arrive_gate(q) for q in range(2)], axis=0).astype(F32)
    gated = jnp.concatenate(readings, axis=0) * silu(gate)

    squares = jnp.sum(gated * gated, axis=1, keepdims=True)
    upper = squares.astype(BF16).astype(F32)
    lane = iota((own, LANES), 1)
    squares = jnp.where(lane % 2 == 0, upper, squares - upper).astype(BF16)
    scaled = jnp.concatenate([(gated * norm_gain[...]).astype(BF16), squares], axis=1)
    at_row, from_row = iota((own, own), 0), iota((own, own), 1)
    turn = (from_row == (at_row % steps) * kids + at_row // steps).astype(F32).astype(BF16)
    scaled = jnp.dot(turn, scaled, preferred_element_type=F32)
    bands, cuts = own // 16, width // LANES
    marks = scaled[:16, width:]
    for r in range(bands):
        band = scaled[r * 16 : (r + 1) * 16]
        for i in range(cuts):
            nrm_all[p, r * cuts + i] = band[:, i * LANES : (i + 1) * LANES].astype(BF16)
        if r > 0:
            marks = jnp.where(iota(marks.shape, 1) < 2 * r, marks, band[:, width:])
    nrm_all[p, bands * cuts] = marks.astype(BF16)

    def nrm_copy(at, target, send, recv):
        return pltpu.make_async_remote_copy(
            src_ref=nrm_all.at[at],
            dst_ref=nrm_all.at[at],
            send_sem=send,
            recv_sem=recv,
            device_id={"particle": target},
            device_id_type=MESH,
        )

    def direct(i):
        target = lax.rem(p + 2 * order[i] + np_, np_)
        return nrm_copy(p, target, nrm_send.at[i], nrm_recv.at[i])

    def forward(i):
        at = lax.rem(p - 2 * order[i] + np_, np_)
        return nrm_copy(at, sibling, fwd_send.at[i], fwd_recv.at[i])

    for i in reversed(range(zs - 1)):
        direct(i).start()
    forward(zs - 1).start()

    adds = lax.dot_general(
        jnp.concatenate(added, axis=0).astype(BF16),
        apart(writes, kids),
        (((0,), (0,)), ((), ())),
        preferred_element_type=F32,
    )
    for k in range(kids):
        for i in range(heads):
            factor = jnp.broadcast_to(
                kept[k : k + 1, i * headdim : i * headdim + 1], (headdim, state)
            )
            fin[k, i] = (
                win[parent[k], i] * factor
                + adds[i * headdim : (i + 1) * headdim, k * state : (k + 1) * state]
            )
    for i in range(3):
        conv_v[i] = at_step(value, steps - 3 + i)
    results = [
        pltpu.make_async_copy(s, d, res_sem.at[i])
        for i, (s, d) in enumerate([(fin, states_o), (conv_v, conv_o)])
    ]
    for copy in results:
        copy.start()

    def dest_of(i, other):
        return chip(-order[i]) * 2 + (1 - c if other else c)

    def out_copy(i, other):
        return pltpu.make_async_remote_copy(
            src_ref=part.at[i, other],
            dst_ref=parts.at[h],
            send_sem=out_send.at[i, other],
            recv_sem=out_recv.at[h],
            device_id={"head": dest_of(i, other)},
            device_id_type=MESH,
        )

    def send_parts(places):
        block = []
        for i, other in places:
            tiles = nrm_all[dest_of(i, other)]
            for r in range(bands):
                block.append(
                    jnp.concatenate([tiles[r * cuts + n] for n in range(cuts)], axis=1)
                )
        product = jnp.dot(
            jnp.concatenate(block, axis=0), wo_v[...], preferred_element_type=F32
        ).astype(BF16)
        for n, (i, other) in enumerate(places):
            for r in range(bands):
                start = n * own + r * 16
                for e in range(cuts):
                    part[i, other, r * cuts + e] = product[
                        start : start + 16, e * LANES : (e + 1) * LANES
                    ]
            part[i, other, bands * cuts] = nrm_all[dest_of(i, other), bands * cuts]
        for i, other in places:
            dest = dest_of(i, other)

            @pl.when(dest != h)
            def _(i=i, other=other):
                out_copy(i, other).start()

            @pl.when(dest == h)
            def _(i=i, other=other):
                parts[h] = part[i, other]

    def take(i):
        at = chip(-order[i]) * 2 + c
        if order[i] != 0:
            nrm_copy(at, sibling, nrm_send.at[i], nrm_recv.at[i]).wait_recv()
            forward(i).start()

    def take_forward(i):
        at = chip(-order[i]) * 2 + 1 - c
        nrm_copy(at, sibling, fwd_send.at[i], fwd_recv.at[i]).wait_recv()

    near = list(range(zs))[::-1]
    for batch, split in BATCHES:
        batch = [near[n] for n in batch]
        for i in batch:
            take(i)
        if split:
            send_parts([(i, 0) for i in batch])
        for i in batch:
            take_forward(i)
        send_parts([(i, o) for i in batch for o in range(split, 2)])

    for m in range(2):
        each(lambda j, m=m: rs_copy(m, j).wait_send())
        each(lambda j, m=m: ag_copy(m, j).wait_send())
    for copy in shifts:
        copy.wait_send()
    for kind in range(3):
        for m in range(2):
            sib_copy(kind, m).wait_send()
    for kind in range(2):
        for i in range(zs - 1):
            z_copy(kind, i).wait_send()
    for q, way in legs:
        far_copy(q, way).wait_send()
        for n in range(2):
            near_copy(q, way, n).wait_send()
    for j in range(1, span):
        mate_copy(j).wait_send()
    for i in range(zs - 1):
        direct(i).wait_send()
    for i in range(zs):
        forward(i).wait_send()
    for copy in results:
        copy.wait()

    totals = [[jnp.zeros((16, LANES), F32) for _ in range(cuts)] for _ in range(bands)]
    for g in range(GROUPS):
        sums = [[jnp.zeros((16, LANES), F32) for _ in range(cuts)] for _ in range(bands)]
        squares = [jnp.zeros((16, 1), F32) for _ in range(bands)]
        for s in range(g * span, (g + 1) * span):

            @pl.when(s != h)
            def _(s=s):
                pltpu.make_async_remote_copy(
                    src_ref=part.at[0, 0],
                    dst_ref=parts.at[s],
                    send_sem=out_send.at[0, 0],
                    recv_sem=out_recv.at[s],
                    device_id={"head": s},
                    device_id_type=MESH,
                ).wait_recv()

            marks = parts[s, bands * cuts].astype(F32)
            for r in range(bands):
                squares[r] = squares[r] + marks[:, 2 * r : 2 * r + 1] + marks[:, 2 * r + 1 : 2 * r + 2]
                for e in range(cuts):
                    sums[r][e] = sums[r][e] + parts[s, r * cuts + e].astype(F32)
        for r in range(bands):
            scale = lax.rsqrt(squares[r] / (width * span) + EPSILON)
            totals[r] = [a + b * scale for a, b in zip(totals[r], sums[r])]
    for r in range(bands):
        answer = jnp.concatenate(totals[r], axis=1)
        each_kid = 16 // steps
        for k in range(each_kid):
            mixed_o[r * each_kid + k] = answer[k * steps : (k + 1) * steps].astype(BF16)
    for i in range(zs):
        for other in range(2):

            @pl.when(dest_of(i, other) != h)
            def _(i=i, other=other):
                out_copy(i, other).wait_send()


def finish(mixed, states, conv, mixed_o, states_o, conv_o, sems):
    pairs = [(states.at[k], states_o.at[k]) for k in range(states.shape[0])]
    pairs += [(mixed, mixed_o), (conv, conv_o)]
    copies = [pltpu.make_async_copy(a, b, sems.at[i]) for i, (a, b) in enumerate(pairs)]
    for copy in copies:
        copy.start()
    for copy in copies:
        copy.wait()


def on_device(
    np_,
    nh,
    counts,
    ssm_state,
    conv_value,
    conv_wread,
    token_ids,
    embedding,
    w_gate,
    w_value,
    w_wread,
    w_step,
    kern_value,
    bias_value,
    kern_wread,
    bias_wread,
    step_bias,
    decay_log,
    skip_gain,
    norm_gain,
    w_output,
):
    kids, heads, headdim, state = ssm_state.shape
    steps = token_ids.shape[1]
    own = kids * steps
    rows = np_ * own
    owned = rows // 2 // nh
    depth, width = w_value.shape
    cols = w_output.shape[1]
    zs = np_ // 2
    span = nh // GROUPS
    taps = kern_value.shape[0]
    tiles = own // 16 * (width // LANES) + 1
    dma = pltpu.SemaphoreType.DMA
    smem = pltpu.SMEM
    vmem = pltpu.VMEM
    scratch = [
        smem((kids,), jnp.int32),
        smem((heads,), F32),
        smem((heads,), F32),
        smem((heads,), F32),
        vmem((steps, np_ * kids), jnp.int32),
        vmem((np_ * kids, 8), jnp.int32),
        vmem((taps, width), F32),
        vmem((1, width), F32),
        vmem((1, 2 * state), F32),
        vmem((1, width), F32),
        vmem(embedding.shape, BF16),
        vmem((depth, width), BF16),
        vmem((depth, width), BF16),
        vmem((depth, state), BF16),
        vmem((heads, depth), BF16),
        vmem((width, cols), BF16),
        vmem((kids, heads, headdim, state), F32),
        vmem((2, 3, kids, width), F32),
        vmem((2, 3, kids, 2 * state), F32),
        vmem((taps, 2 * state), F32),
        vmem((width, kids * state), BF16),
        vmem((3, kids, width), F32),
        vmem((3, kids, 2 * state), F32),
        vmem((2, nh, owned, depth), BF16),
        vmem((2, nh - 1, owned, depth), BF16),
        vmem((2, nh, owned, depth), BF16),
        vmem((2, zs, own, LANES), BF16),
        vmem((2, zs, own, width), BF16),
        vmem((2, zs, 2, own // 2, width), BF16),
        vmem((zs, own, LANES), BF16),
        vmem((zs, own, width), BF16),
        vmem((zs, 2, own // 2, width), BF16),
        vmem((zs - 1, own, LANES), BF16),
        vmem((zs - 1, own, width), BF16),
        vmem((2, 2, 2, own // 2, width), BF16),
        vmem((2, 2, 2, own // 2, width), BF16),
        vmem((zs - 1, own, LANES), BF16),
        vmem((zs - 1, own, width), BF16),
        vmem((2, 2, 2, own // 2, width), BF16),
        vmem((2, 2, 2, own // 2, width), BF16),
        vmem((span, own, LANES), BF16),
        vmem((np_, tiles, 16, LANES), BF16),
        vmem((zs, 2, tiles, 16, LANES), BF16),
        vmem((nh, tiles, 16, LANES), BF16),
        vmem(ssm_state.shape, F32),
        vmem((3, kids, width), F32),
        dma,
        dma((EMB_PIECES,)),
        dma((20,)),
        dma((4,)),
        dma((4,)),
        dma((2, nh - 1)),
        dma((2, nh - 1)),
        dma((2, nh - 1)),
        dma((2, nh - 1)),
        dma((3, 2)),
        dma((3, 2)),
        dma((2, zs - 1)),
        dma((2, zs - 1)),
        dma((2, 2)),
        dma((2, 2)),
        dma((2, 2, 2)),
        dma((2, 2, 2)),
        dma((span - 1,)),
        dma((span - 1,)),
        dma((zs - 1,)),
        dma((zs - 1,)),
        dma((zs,)),
        dma((zs,)),
        dma((zs, 2)),
        dma((nh,)),
        dma((2,)),
    ]
    hbm = pl.BlockSpec(memory_space=pltpu.HBM)
    limit = 40 * 1024 * 1024
    shape = jax.ShapeDtypeStruct
    operands = (        counts,
        step_bias,
        decay_log,
        skip_gain,
        token_ids.T,
        kern_value,
        bias_value.reshape(1, -1),
        kern_wread,
        bias_wread.reshape(1, -1),
        norm_gain.reshape(1, -1),
        ssm_state,
        conv_value.transpose(1, 0, 2),
        conv_wread.transpose(1, 0, 2),
        embedding,
        w_gate,
        w_value,
        w_wread,
        w_step.T,
        w_output,
    )
    operands = [pltpu.with_memory_space_constraint(a, pltpu.HBM) for a in operands]
    results = pl.pallas_call(
        functools.partial(fused, np_, nh),
        out_shape=(
            shape((kids, steps, cols), BF16),
            shape(ssm_state.shape, F32),
            shape((3, kids, width), F32),
        ),
        in_specs=[hbm] * 19,
        out_specs=(pl.BlockSpec(memory_space=pltpu.VMEM),)
        + (pl.BlockSpec(memory_space=pl.ANY),) * 2,
        scratch_shapes=scratch,
        compiler_params=pltpu.CompilerParams(
            collective_id=0, has_side_effects=True, vmem_limit_bytes=limit
        ),
    )(*operands)
    mixed, final_state, final_conv = pl.pallas_call(
        finish,
        out_shape=(
            shape((kids, steps, cols), BF16),
            shape(ssm_state.shape, F32),
            shape((3, kids, width), F32),
        ),
        in_specs=[pl.BlockSpec(memory_space=pltpu.VMEM)] * 3,
        out_specs=(hbm,) * 3,
        scratch_shapes=[dma((kids + 2,))],
        compiler_params=pltpu.CompilerParams(vmem_limit_bytes=limit),
    )(*results)
    return mixed, final_state, final_conv.transpose(1, 0, 2)


def solution(mesh):
    return jax.shard_map(
        functools.partial(on_device, mesh.shape["particle"], mesh.shape["head"]),
        mesh=mesh,
        in_specs=(
            P("particle"),
            P("particle", "head", None, None),
            P("particle", None, "head"),
            P("particle", None, None),
            P(),
            P("head", "particle"),
            P("particle", "head"),
            P("particle", "head"),
            P("particle", None),
            P("particle", "head"),
            P(None, "head"),
            P("head"),
            P(),
            P(),
            P("head"),
            P("head"),
            P("head"),
            P("head"),
            P("head", "particle"),
        ),
        out_specs=(
            P("head", None, "particle"),
            P("particle", "head", None, None),
            P("particle", None, "head"),
        ),
        check_vma=False,
    )
```

```python
import functools
import math

import jax
import jax.numpy as jnp
from jax import lax
from jax.experimental import pallas as pl
from jax.experimental.pallas import tpu as pltpu
from jax.sharding import PartitionSpec as P

GROUPS = 4
EPSILON = 1e-05
MESH = pl.DeviceIdType.MESH
F32 = jnp.float32
BF16 = jnp.bfloat16
LANES = 128
EMB_PIECES = 4
BATCHES = (((0, 1, 2), 0), ((3, 4), 0), ((5, 6, 7), 1))


def silu(x):
    return x * (1.0 / (1.0 + jnp.exp(-x)))


def softplus(x):
    return jnp.maximum(x, 0.0) + jnp.log1p(jnp.exp(-jnp.abs(x)))


def iota(shape, axis):
    return lax.broadcasted_iota(jnp.int32, shape, axis)


def keep_rows(kids, counts):
    counted = counts[0]
    for i in range(1, kids - 1):
        counted = counted + counts[i]
    running = kids - counted
    marks = [running]
    for i in range(kids - 1):
        running = running + counts[i]
        marks.append(running)
    parent = []
    for k in range(kids):
        at = jnp.int32(0)
        for mark in marks:
            at = at + (mark <= k).astype(jnp.int32)
        parent.append(jnp.minimum(at, kids - 1))
    return parent


def apart(blocks, kids):
    whole = jnp.concatenate(blocks, axis=0)
    child = iota(whole.shape, 0) % kids
    return jnp.concatenate(
        [jnp.where(child == k, whole, 0.0) for k in range(kids)], axis=1
    ).astype(BF16)


def fused(
    np_,
    nh,
    counts_h,
    step_bias_h,
    decay_log_h,
    skip_gain_h,
    tok_h,
    kern_value_h,
    bias_value_h,
    kern_wread,
    bias_wread,
    norm_gain_h,
    ssm,
    conv_value,
    conv_wread,
    emb,
    w_gate,
    w_value,
    w_wread,
    w_step,
    w_output,
    mixed_o,
    states_o,
    conv_o,
    counts,
    step_bias,
    decay_log,
    skip_gain,
    tok,
    ids_s,
    kern_value,
    bias_value,
    bw_v,
    norm_gain,
    emb_v,
    wg_v,
    wv_v,
    ww_v,
    ws_v,
    wo_v,
    win,
    cwin,
    wwin,
    kw_v,
    sbf,
    hist,
    whist,
    tok_part,
    tok_recv,
    tok_all,
    term_w,
    term_v,
    term_g,
    sib_w,
    sib_v,
    sib_g,
    out_w,
    out_v,
    out_far,
    out_near,
    in_w,
    in_v,
    in_far,
    in_near,
    quarter,
    nrm_all,
    part,
    parts,
    fin,
    conv_v,
    tok_sem,
    emb_sem,
    loc_sem,
    shift_send,
    shift_recv,
    rs_send,
    rs_recv,
    ag_send,
    ag_recv,
    sib_send,
    sib_recv,
    z_send,
    z_recv,
    far_send,
    far_recv,
    near_send,
    near_recv,
    mate_send,
    mate_recv,
    nrm_send,
    nrm_recv,
    fwd_send,
    fwd_recv,
    out_send,
    out_recv,
    res_sem,
):
    p = lax.axis_index("particle")
    h = lax.axis_index("head")
    zs = np_ // 2
    z = p // 2
    c = p % 2
    sibling = z * 2 + 1 - c
    kids = counts.shape[0]
    steps = tok.shape[0]
    own = kids * steps
    rows = np_ * own
    width = wv_v.shape[1]
    state = ssm.shape[3]
    heads = ssm.shape[1]
    headdim = ssm.shape[2]
    vocab = emb.shape[0]
    span = nh // GROUPS
    group, mate = h // span, h % span
    share = 2 * state // span
    half = rows // 2
    owned = half // nh
    reach = zs // 2
    order = [reach]
    for d in range(reach - 1, 0, -1):
        order += [d, -d]
    order.append(0)

    def chip(d):
        return lax.rem(z + d + zs, zs)

    tok_copy = pltpu.make_async_copy(tok_h, tok, tok_sem)
    tok_copy.start()
    piece = vocab // EMB_PIECES
    emb_copies = [
        pltpu.make_async_copy(
            emb.at[pl.ds(i * piece, piece)], emb_v.at[pl.ds(i * piece, piece)], emb_sem.at[i]
        )
        for i in range(EMB_PIECES)
    ]
    for copy in emb_copies:
        copy.start()

    barrier = pltpu.get_barrier_semaphore()
    mates = [{"head": lax.rem(h + j, nh)} for j in range(1, nh)]
    mates += [{"particle": lax.rem(p + 2 * j, np_)} for j in range(1, zs)]
    mates += [{"particle": sibling}, {"particle": lax.rem(p + np_ - 1 + 2 * c, np_)}]
    for other in mates:
        pl.semaphore_signal(barrier, inc=1, device_id=other, device_id_type=MESH)
    at_write = pl.ds(pl.multiple_of(group * state, state), state)
    at_read = pl.ds(pl.multiple_of((GROUPS + group) * state, state), state)
    side = mate // (span // 2)
    at_share = pl.ds(pl.multiple_of((side * GROUPS + group) * state, state), state)
    lo, hi = pl.ds(0, state), pl.ds(state, state)
    pairs = [
        (ssm.at[pl.ds(0, kids - 1)], win.at[pl.ds(1, kids - 1)]),
        (conv_value, cwin.at[1]),
        (conv_wread.at[:, :, at_write], wwin.at[1, :, :, lo]),
        (conv_wread.at[:, :, at_read], wwin.at[1, :, :, hi]),
        (counts_h, counts),
        (w_wread.at[:, at_share], ww_v),
        (w_step, ws_v),
        (w_value, wv_v),
        (w_gate, wg_v),
        (kern_wread.at[:, at_write], kw_v.at[:, lo]),
        (kern_wread.at[:, at_read], kw_v.at[:, hi]),
        (w_output, wo_v),
        (step_bias_h, step_bias),
        (decay_log_h, decay_log),
        (skip_gain_h, skip_gain),
        (kern_value_h, kern_value),
        (bias_value_h, bias_value),
        (norm_gain_h, norm_gain),
        (bias_wread.at[:, at_write], bw_v.at[:, lo]),
        (bias_wread.at[:, at_read], bw_v.at[:, hi]),
    ]
    loads = [pltpu.make_async_copy(s, d, loc_sem.at[i]) for i, (s, d) in enumerate(pairs)]

    tok_copy.wait()
    ids_t = jnp.concatenate([tok[...], jnp.zeros((8 - steps, np_ * kids), jnp.int32)], axis=0).T
    ids_s[...] = ids_t - h * vocab

    def lookup(m):
        column = []
        for d in order[m * reach : (m + 1) * reach]:
            pair = ids_s[pl.ds(pl.multiple_of(chip(d) * 2 * kids, 2 * kids), 2 * kids), :]
            for core in range(2):
                for t in range(steps):
                    column.append(pair[core * kids : (core + 1) * kids, t : t + 1])
        ids = jnp.concatenate(column, axis=0)
        total = None
        for i in range(EMB_PIECES):
            if m == 0:
                emb_copies[i].wait()
            hot = jnp.where(ids - i * piece == iota((half, piece), 1), 1.0, 0.0).astype(BF16)
            term = jnp.dot(hot, emb_v[pl.ds(i * piece, piece)], preferred_element_type=F32)
            total = term if total is None else total + term
        tok_part[m] = total.astype(BF16).reshape(nh, owned, -1)

    side_x = math.isqrt(nh)
    side_y = nh // side_x
    offsets = [(a, b) for a in range(side_x) for b in range(side_y) if a or b]
    offsets.sort(key=lambda o: -min(o[0], side_x - o[0]) - min(o[1], side_y - o[1]))

    def at_offset(j, way):
        a, b = offsets[j - 1]
        x = lax.rem(h // side_y + way * a + side_x, side_x)
        y = lax.rem(h % side_y + way * b + side_y, side_y)
        return x * side_y + y

    def rs_copy(m, j):
        dest = at_offset(j, 1)
        return pltpu.make_async_remote_copy(
            src_ref=tok_part.at[m, dest],
            dst_ref=tok_recv.at[m, j - 1],
            send_sem=rs_send.at[m, j - 1],
            recv_sem=rs_recv.at[m, j - 1],
            device_id={"head": dest},
            device_id_type=MESH,
        )

    def ag_copy(m, j):
        return pltpu.make_async_remote_copy(
            src_ref=tok_all.at[m, h],
            dst_ref=tok_all.at[m, h],
            send_sem=ag_send.at[m, j - 1],
            recv_sem=ag_recv.at[m, j - 1],
            device_id={"head": at_offset(j, 1)},
            device_id_type=MESH,
        )

    def ag_back(m, j):
        source = at_offset(j, -1)
        return pltpu.make_async_remote_copy(
            src_ref=tok_all.at[m, h],
            dst_ref=tok_all.at[m, source],
            send_sem=ag_send.at[m, j - 1],
            recv_sem=ag_recv.at[m, j - 1],
            device_id={"head": source},
            device_id_type=MESH,
        )

    def each(do):
        for j in range(1, nh):
            do(j)

    lookup(0)
    pl.semaphore_wait(barrier, len(mates))
    each(lambda j: rs_copy(0, j).start())
    lookup(1)
    each(lambda j: rs_copy(1, j).start())
    for copy in loads:
        copy.start()

    above = lax.rem(p + 1, np_)
    shift_pairs = [
        (ssm.at[kids - 1], win.at[0]),
        (conv_value, cwin.at[0]),
        (conv_wread.at[:, :, at_write], wwin.at[0, :, :, lo]),
        (conv_wread.at[:, :, at_read], wwin.at[0, :, :, hi]),
    ]
    shifts = [
        pltpu.make_async_remote_copy(
            src_ref=s,
            dst_ref=d,
            send_sem=shift_send.at[i],
            recv_sem=shift_recv.at[i],
            device_id={"particle": above},
            device_id_type=MESH,
        )
        for i, (s, d) in enumerate(shift_pairs)
    ]
    for copy in shifts:
        copy.start()

    for m in range(2):
        each(lambda j, m=m: rs_copy(m, j).wait_recv())
        shared = tok_part[m, h]
        for s in range(nh - 1):
            shared = shared + tok_recv[m, s]
        tok_all[m, h] = shared
        each(lambda j, m=m: ag_copy(m, j).start())

    for copy in loads[:5]:
        copy.wait()
    parent = keep_rows(kids, counts)
    for copy in shifts:
        copy.wait_recv()
    for k in range(kids):
        sbf[:, pl.ds(k * state, state)] = win[parent[k]].reshape(width, state).astype(BF16)
        here = jnp.minimum(parent[k], 1)
        row = pl.ds(jnp.where(parent[k] == 0, kids - 1, parent[k] - 1), 1)
        for tap in range(3):
            hist[tap, pl.ds(k, 1), :] = cwin[here, tap, row, :]
            whist[tap, pl.ds(k, 1), :] = wwin[here, tap, row, :]
    for copy in loads[5:]:
        copy.wait()

    kinds = [
        (term_w, sib_w, out_w, in_w),
        (term_v, sib_v, out_v, in_v),
        (term_g, sib_g),
    ]

    def sib_copy(kind, m):
        source, target = kinds[kind][:2]
        return pltpu.make_async_remote_copy(
            src_ref=source.at[1 - c, pl.ds(m * reach, reach)],
            dst_ref=target.at[pl.ds(m * reach, reach)],
            send_sem=sib_send.at[kind, m],
            recv_sem=sib_recv.at[kind, m],
            device_id={"particle": sibling},
            device_id_type=MESH,
        )

    def along(d):
        return {"particle": lax.rem(p + 2 * d + np_, np_)}

    def z_copy(kind, i):
        _, _, out, back = kinds[kind]
        return pltpu.make_async_remote_copy(
            src_ref=out.at[i],
            dst_ref=back.at[i],
            send_sem=z_send.at[kind, i],
            recv_sem=z_recv.at[kind, i],
            device_id=along(order[i]),
            device_id_type=MESH,
        )

    def place(kind, m, terms):
        source = kinds[kind][0]
        for b in range(2 * reach):
            block = terms[b * own : (b + 1) * own].astype(BF16)
            source[b % 2, m * reach + b // 2] = block.reshape(source.shape[2:])
        sib_copy(kind, m).start()

    def chip_sum(kind, i):
        return kinds[kind][0][c, i].astype(F32) + kinds[kind][1][i].astype(F32)

    def send_sums(kind, which):
        for i in which:
            kinds[kind][2][i] = chip_sum(kind, i).astype(BF16)
            z_copy(kind, i).start()

    def arrive(kind):
        total = chip_sum(kind, zs - 1)
        for i in range(zs - 1):
            z_copy(kind, i).wait_recv()
            total = total + kinds[kind][3][i].astype(F32)
        return total.astype(BF16)

    def gate_sum(d, q):
        i = order.index(d)
        return term_g[c, i, q].astype(F32) + sib_g[i, q].astype(F32)

    def whole(q, way):
        return (way == 1) == (q == 0)

    def far_copy(q, way):
        side = (1 - way) // 2
        cut = pl.ds(0, 2) if whole(q, way) else pl.ds(1, 1)
        return pltpu.make_async_remote_copy(
            src_ref=out_far.at[q, side, cut],
            dst_ref=in_far.at[q, side, cut],
            send_sem=far_send.at[q, side],
            recv_sem=far_recv.at[q, side],
            device_id=along(2 * way),
            device_id_type=MESH,
        )

    def near_copy(q, way, n):
        side = (1 - way) // 2
        return pltpu.make_async_remote_copy(
            src_ref=out_near.at[q, side, n],
            dst_ref=in_near.at[q, side, n],
            send_sem=near_send.at[q, side, n],
            recv_sem=near_recv.at[q, side, n],
            device_id=along((2 - n) * way),
            device_id_type=MESH,
        )

    legs = [(q, way) for q in range(2) for way in (1, -1)]

    for m in range(2):
        each(lambda j, m=m: ag_back(m, j).wait_recv())
        tokens = tok_all[m].reshape(half, -1)
        place(2, m, jnp.dot(tokens, wg_v[...], preferred_element_type=F32))
        matrices = jnp.dot(tokens, ww_v[...], preferred_element_type=F32)
        rate = lax.dot_general(
            tokens, ws_v[...], (((1,), (1,)), ((), ())), preferred_element_type=F32
        )
        pads = [jnp.zeros((half, n), F32) for n in (share, LANES - share - heads)]
        rate = jnp.concatenate([pads[0], rate, pads[1]], axis=1)
        turned = jnp.concatenate([matrices[:, share:], matrices[:, :share]], axis=1)
        matrices = jnp.where(mate % (span // 2) == 0, matrices, turned)
        place(0, m, jnp.where(iota((half, LANES), 1) < share, matrices, rate))
        sib_copy(2, m).wait_recv()
        if m == 0:
            for q, way in legs:
                side = (1 - way) // 2
                if whole(q, way):
                    out_far[q, side, 0] = gate_sum(reach, q).astype(BF16)
                out_far[q, side, 1] = gate_sum(way * (reach - 1), q).astype(BF16)
                far_copy(q, way).start()
        place(1, m, jnp.dot(tokens, wv_v[...], preferred_element_type=F32))
        sib_copy(0, m).wait_recv()
        send_sums(0, range(m * reach, min((m + 1) * reach, zs - 1)))
        sib_copy(1, m).wait_recv()
    send_sums(1, range(zs - 1))
    for q, way in legs:
        side = (1 - way) // 2
        far_copy(q, way).wait_recv()
        for n in range(2):
            term = gate_sum(way * (2 - n), q)
            if n == 1 or whole(q, way):
                term = term + in_far[q, side, n].astype(F32)
            out_near[q, side, n] = term.astype(BF16)
            near_copy(q, way, n).start()

    def arrive_gate(q):
        total = gate_sum(0, q)
        for side, way in enumerate((1, -1)):
            for n in range(2):
                near_copy(q, way, n).wait_recv()
                total = total + in_near[q, side, n].astype(F32)
        return total.astype(BF16)

    narrow = arrive(0)
    quarter[mate] = narrow

    def mate_copy(j):
        return pltpu.make_async_remote_copy(
            src_ref=quarter.at[mate],
            dst_ref=quarter.at[mate],
            send_sem=mate_send.at[j - 1],
            recv_sem=mate_recv.at[j - 1],
            device_id={"head": group * span + lax.rem(mate + j, span)},
            device_id_type=MESH,
        )

    def mate_back(j):
        source = lax.rem(mate + span - j, span)
        return pltpu.make_async_remote_copy(
            src_ref=quarter.at[mate],
            dst_ref=quarter.at[source],
            send_sem=mate_send.at[j - 1],
            recv_sem=mate_recv.at[j - 1],
            device_id={"head": group * span + source},
            device_id_type=MESH,
        )

    for j in range(1, span):
        mate_copy(j).start()

    def at_step(a, t):
        return a[t * kids : (t + 1) * kids]

    spread = (
        iota((LANES, width), 1) // headdim + share == iota((LANES, width), 0)
    ).astype(F32)
    rates = jnp.dot(narrow, spread.astype(BF16), preferred_element_type=F32)
    lane_head = iota((1, width), 1) // headdim

    def per_head(ref):
        out = jnp.zeros((1, width), F32)
        for i in range(heads):
            out = jnp.where(lane_head == i, ref[i], out)
        return out

    step_size = softplus(rates + per_head(step_bias))
    decay = jnp.exp(-step_size * jnp.exp(per_head(decay_log)))
    skip = per_head(skip_gain)

    def convolve(past, current, kern, bias):
        seq = [past[i] for i in range(3)] + [at_step(current, t) for t in range(steps)]
        out = []
        for t in range(steps):
            a = seq[t] * kern[0:1]
            for i in range(1, 4):
                a = a + seq[t + i] * kern[i : i + 1]
            out.append(silu(a + bias))
        return out

    for j in range(1, span):
        mate_back(j).wait_recv()
    wread = jnp.concatenate([quarter[i].astype(F32)[:, :share] for i in range(span)], axis=1)
    conv_w = convolve(whist, wread, kw_v[...], bw_v[...])
    writes = [a[:, :state] for a in conv_w]
    reads = [a[:, state:] for a in conv_w]
    first = lax.dot_general(
        apart(reads, kids), sbf[...], (((1,), (1,)), ((), ())), preferred_element_type=F32
    )
    kept = None
    starts = []
    for t in range(steps):
        now = at_step(decay, t)
        kept = now if kept is None else kept * now
        starts.append(kept * at_step(first, t))
    match = {
        (u, t): jnp.sum(writes[u] * reads[t], axis=1, keepdims=True)
        for t in range(steps)
        for u in range(t + 1)
    }
    value = arrive(1).astype(F32)
    conv = convolve(hist, value, kern_value[...], bias_value[...])

    added = []
    readings = []
    for t in range(steps):
        now = at_step(decay, t)
        added = [a * now for a in added] + [at_step(step_size, t) * conv[t]]
        reading = starts[t] + skip * conv[t]
        for u in range(t + 1):
            reading = reading + added[u] * match[u, t]
        readings.append(reading)
    gate = jnp.concatenate([arrive_gate(q) for q in range(2)], axis=0).astype(F32)
    gated = jnp.concatenate(readings, axis=0) * silu(gate)

    scaled = (gated * norm_gain[...]).astype(BF16)
    at_row, from_row = iota((own, own), 0), iota((own, own), 1)
    turn = (from_row == (at_row % steps) * kids + at_row // steps).astype(F32).astype(BF16)
    scaled = jnp.dot(turn, scaled, preferred_element_type=F32)
    bands, cuts = own // 16, width // LANES
    for r in range(bands):
        for i in range(cuts):
            tile = scaled[r * 16 : (r + 1) * 16, i * LANES : (i + 1) * LANES]
            nrm_all[p, r * cuts + i] = tile.astype(BF16)

    def nrm_copy(at, target, send, recv):
        return pltpu.make_async_remote_copy(
            src_ref=nrm_all.at[at],
            dst_ref=nrm_all.at[at],
            send_sem=send,
            recv_sem=recv,
            device_id={"particle": target},
            device_id_type=MESH,
        )

    def direct(i):
        target = lax.rem(p + 2 * order[i] + np_, np_)
        return nrm_copy(p, target, nrm_send.at[i], nrm_recv.at[i])

    def forward(i):
        at = lax.rem(p - 2 * order[i] + np_, np_)
        return nrm_copy(at, sibling, fwd_send.at[i], fwd_recv.at[i])

    for i in reversed(range(zs - 1)):
        direct(i).start()
    forward(zs - 1).start()

    adds = lax.dot_general(
        jnp.concatenate(added, axis=0).astype(BF16),
        apart(writes, kids),
        (((0,), (0,)), ((), ())),
        preferred_element_type=F32,
    )
    for k in range(kids):
        for i in range(heads):
            factor = jnp.broadcast_to(
                kept[k : k + 1, i * headdim : i * headdim + 1], (headdim, state)
            )
            fin[k, i] = (
                win[parent[k], i] * factor
                + adds[i * headdim : (i + 1) * headdim, k * state : (k + 1) * state]
            )
    for i in range(3):
        conv_v[i] = at_step(value, steps - 3 + i)
    results = [
        pltpu.make_async_copy(s, d, res_sem.at[i])
        for i, (s, d) in enumerate([(fin, states_o), (conv_v, conv_o)])
    ]
    for copy in results:
        copy.start()

    def dest_of(i, other):
        return chip(-order[i]) * 2 + (1 - c if other else c)

    def out_copy(i, other):
        return pltpu.make_async_remote_copy(
            src_ref=part.at[i, other],
            dst_ref=parts.at[h],
            send_sem=out_send.at[i, other],
            recv_sem=out_recv.at[h],
            device_id={"head": dest_of(i, other)},
            device_id_type=MESH,
        )

    def send_parts(places):
        block = []
        for i, other in places:
            tiles = nrm_all[dest_of(i, other)]
            for r in range(bands):
                block.append(
                    jnp.concatenate([tiles[r * cuts + n] for n in range(cuts)], axis=1)
                )
        block = jnp.concatenate(block, axis=0)
        product = jnp.dot(block, wo_v[...], preferred_element_type=F32).astype(BF16)
        plain = block.astype(F32) * ungain
        squares = jnp.sum(plain * plain, axis=1, keepdims=True)
        upper = squares.astype(BF16).astype(F32)
        lane = iota((block.shape[0], LANES), 1)
        squares = jnp.where(lane % 2 == 0, upper, squares - upper)
        for n, (i, other) in enumerate(places):
            marks = squares[n * own : n * own + 16]
            for r in range(1, bands):
                start = n * own + r * 16
                marks = jnp.where(lane[:16] < 2 * r, marks, squares[start : start + 16])
            part[i, other, bands * cuts] = marks.astype(BF16)
            for r in range(bands):
                start = n * own + r * 16
                for e in range(cuts):
                    part[i, other, r * cuts + e] = product[
                        start : start + 16, e * LANES : (e + 1) * LANES
                    ]
        for i, other in places:
            dest = dest_of(i, other)

            @pl.when(dest != h)
            def _(i=i, other=other):
                out_copy(i, other).start()

            @pl.when(dest == h)
            def _(i=i, other=other):
                parts[h] = part[i, other]

    def take(i):
        at = chip(-order[i]) * 2 + c
        if order[i] != 0:
            nrm_copy(at, sibling, nrm_send.at[i], nrm_recv.at[i]).wait_recv()
            forward(i).start()

    def take_forward(i):
        at = chip(-order[i]) * 2 + 1 - c
        nrm_copy(at, sibling, fwd_send.at[i], fwd_recv.at[i]).wait_recv()

    ungain = 1.0 / norm_gain[...]
    near = list(range(zs))[::-1]
    for batch, split in BATCHES:
        batch = [near[n] for n in batch]
        for i in batch:
            take(i)
        if split:
            send_parts([(i, 0) for i in batch])
        for i in batch:
            take_forward(i)
        send_parts([(i, o) for i in batch for o in range(split, 2)])

    for m in range(2):
        each(lambda j, m=m: rs_copy(m, j).wait_send())
        each(lambda j, m=m: ag_copy(m, j).wait_send())
    for copy in shifts:
        copy.wait_send()
    for kind in range(3):
        for m in range(2):
            sib_copy(kind, m).wait_send()
    for kind in range(2):
        for i in range(zs - 1):
            z_copy(kind, i).wait_send()
    for q, way in legs:
        far_copy(q, way).wait_send()
        for n in range(2):
            near_copy(q, way, n).wait_send()
    for j in range(1, span):
        mate_copy(j).wait_send()
    for i in range(zs - 1):
        direct(i).wait_send()
    for i in range(zs):
        forward(i).wait_send()
    for copy in results:
        copy.wait()

    totals = [[jnp.zeros((16, LANES), F32) for _ in range(cuts)] for _ in range(bands)]
    for g in range(GROUPS):
        sums = [[jnp.zeros((16, LANES), F32) for _ in range(cuts)] for _ in range(bands)]
        squares = [jnp.zeros((16, 1), F32) for _ in range(bands)]
        for s in range(g * span, (g + 1) * span):

            @pl.when(s != h)
            def _(s=s):
                pltpu.make_async_remote_copy(
                    src_ref=part.at[0, 0],
                    dst_ref=parts.at[s],
                    send_sem=out_send.at[0, 0],
                    recv_sem=out_recv.at[s],
                    device_id={"head": s},
                    device_id_type=MESH,
                ).wait_recv()

            marks = parts[s, bands * cuts].astype(F32)
            for r in range(bands):
                squares[r] = squares[r] + marks[:, 2 * r : 2 * r + 1] + marks[:, 2 * r + 1 : 2 * r + 2]
                for e in range(cuts):
                    sums[r][e] = sums[r][e] + parts[s, r * cuts + e].astype(F32)
        for r in range(bands):
            scale = lax.rsqrt(squares[r] / (width * span) + EPSILON)
            totals[r] = [a + b * scale for a, b in zip(totals[r], sums[r])]
    for r in range(bands):
        answer = jnp.concatenate(totals[r], axis=1)
        each_kid = 16 // steps
        for k in range(each_kid):
            mixed_o[r * each_kid + k] = answer[k * steps : (k + 1) * steps].astype(BF16)
    for i in range(zs):
        for other in range(2):

            @pl.when(dest_of(i, other) != h)
            def _(i=i, other=other):
                out_copy(i, other).wait_send()


def finish(mixed, states, conv, mixed_o, states_o, conv_o, sems):
    pairs = [(states.at[k], states_o.at[k]) for k in range(states.shape[0])]
    pairs += [(mixed, mixed_o), (conv, conv_o)]
    copies = [pltpu.make_async_copy(a, b, sems.at[i]) for i, (a, b) in enumerate(pairs)]
    for copy in copies:
        copy.start()
    for copy in copies:
        copy.wait()


def on_device(
    np_,
    nh,
    counts,
    ssm_state,
    conv_value,
    conv_wread,
    token_ids,
    embedding,
    w_gate,
    w_value,
    w_wread,
    w_step,
    kern_value,
    bias_value,
    kern_wread,
    bias_wread,
    step_bias,
    decay_log,
    skip_gain,
    norm_gain,
    w_output,
):
    kids, heads, headdim, state = ssm_state.shape
    steps = token_ids.shape[1]
    own = kids * steps
    rows = np_ * own
    owned = rows // 2 // nh
    depth, width = w_value.shape
    cols = w_output.shape[1]
    zs = np_ // 2
    span = nh // GROUPS
    taps = kern_value.shape[0]
    tiles = own // 16 * (width // LANES) + 1
    dma = pltpu.SemaphoreType.DMA
    smem = pltpu.SMEM
    vmem = pltpu.VMEM
    scratch = [
        smem((kids,), jnp.int32),
        smem((heads,), F32),
        smem((heads,), F32),
        smem((heads,), F32),
        vmem((steps, np_ * kids), jnp.int32),
        vmem((np_ * kids, 8), jnp.int32),
        vmem((taps, width), F32),
        vmem((1, width), F32),
        vmem((1, 2 * state), F32),
        vmem((1, width), F32),
        vmem(embedding.shape, BF16),
        vmem((depth, width), BF16),
        vmem((depth, width), BF16),
        vmem((depth, state), BF16),
        vmem((heads, depth), BF16),
        vmem((width, cols), BF16),
        vmem((kids, heads, headdim, state), F32),
        vmem((2, 3, kids, width), F32),
        vmem((2, 3, kids, 2 * state), F32),
        vmem((taps, 2 * state), F32),
        vmem((width, kids * state), BF16),
        vmem((3, kids, width), F32),
        vmem((3, kids, 2 * state), F32),
        vmem((2, nh, owned, depth), BF16),
        vmem((2, nh - 1, owned, depth), BF16),
        vmem((2, nh, owned, depth), BF16),
        vmem((2, zs, own, LANES), BF16),
        vmem((2, zs, own, width), BF16),
        vmem((2, zs, 2, own // 2, width), BF16),
        vmem((zs, own, LANES), BF16),
        vmem((zs, own, width), BF16),
        vmem((zs, 2, own // 2, width), BF16),
        vmem((zs - 1, own, LANES), BF16),
        vmem((zs - 1, own, width), BF16),
        vmem((2, 2, 2, own // 2, width), BF16),
        vmem((2, 2, 2, own // 2, width), BF16),
        vmem((zs - 1, own, LANES), BF16),
        vmem((zs - 1, own, width), BF16),
        vmem((2, 2, 2, own // 2, width), BF16),
        vmem((2, 2, 2, own // 2, width), BF16),
        vmem((span, own, LANES), BF16),
        vmem((np_, tiles - 1, 16, LANES), BF16),
        vmem((zs, 2, tiles, 16, LANES), BF16),
        vmem((nh, tiles, 16, LANES), BF16),
        vmem(ssm_state.shape, F32),
        vmem((3, kids, width), F32),
        dma,
        dma((EMB_PIECES,)),
        dma((20,)),
        dma((4,)),
        dma((4,)),
        dma((2, nh - 1)),
        dma((2, nh - 1)),
        dma((2, nh - 1)),
        dma((2, nh - 1)),
        dma((3, 2)),
        dma((3, 2)),
        dma((2, zs - 1)),
        dma((2, zs - 1)),
        dma((2, 2)),
        dma((2, 2)),
        dma((2, 2, 2)),
        dma((2, 2, 2)),
        dma((span - 1,)),
        dma((span - 1,)),
        dma((zs - 1,)),
        dma((zs - 1,)),
        dma((zs,)),
        dma((zs,)),
        dma((zs, 2)),
        dma((nh,)),
        dma((2,)),
    ]
    hbm = pl.BlockSpec(memory_space=pltpu.HBM)
    limit = 40 * 1024 * 1024
    shape = jax.ShapeDtypeStruct
    operands = (        counts,
        step_bias,
        decay_log,
        skip_gain,
        token_ids.T,
        kern_value,
        bias_value.reshape(1, -1),
        kern_wread,
        bias_wread.reshape(1, -1),
        norm_gain.reshape(1, -1),
        ssm_state,
        conv_value.transpose(1, 0, 2),
        conv_wread.transpose(1, 0, 2),
        embedding,
        w_gate,
        w_value,
        w_wread,
        w_step.T,
        w_output,
    )
    operands = [pltpu.with_memory_space_constraint(a, pltpu.HBM) for a in operands]
    results = pl.pallas_call(
        functools.partial(fused, np_, nh),
        out_shape=(
            shape((kids, steps, cols), BF16),
            shape(ssm_state.shape, F32),
            shape((3, kids, width), F32),
        ),
        in_specs=[hbm] * 19,
        out_specs=(pl.BlockSpec(memory_space=pltpu.VMEM),)
        + (pl.BlockSpec(memory_space=pl.ANY),) * 2,
        scratch_shapes=scratch,
        compiler_params=pltpu.CompilerParams(
            collective_id=0, has_side_effects=True, vmem_limit_bytes=limit
        ),
    )(*operands)
    mixed, final_state, final_conv = pl.pallas_call(
        finish,
        out_shape=(
            shape((kids, steps, cols), BF16),
            shape(ssm_state.shape, F32),
            shape((3, kids, width), F32),
        ),
        in_specs=[pl.BlockSpec(memory_space=pltpu.VMEM)] * 3,
        out_specs=(hbm,) * 3,
        scratch_shapes=[dma((kids + 2,))],
        compiler_params=pltpu.CompilerParams(vmem_limit_bytes=limit),
    )(*results)
    return mixed, final_state, final_conv.transpose(1, 0, 2)


def solution(mesh):
    return jax.shard_map(
        functools.partial(on_device, mesh.shape["particle"], mesh.shape["head"]),
        mesh=mesh,
        in_specs=(
            P("particle"),
            P("particle", "head", None, None),
            P("particle", None, "head"),
            P("particle", None, None),
            P(),
            P("head", "particle"),
            P("particle", "head"),
            P("particle", "head"),
            P("particle", None),
            P("particle", "head"),
            P(None, "head"),
            P("head"),
            P(),
            P(),
            P("head"),
            P("head"),
            P("head"),
            P("head"),
            P("head", "particle"),
        ),
        out_specs=(
            P("head", None, "particle"),
            P("particle", "head", None, None),
            P("particle", None, "head"),
        ),
        check_vma=False,
    )
```

```python
import functools
import math

import jax
import jax.numpy as jnp
from jax import lax
from jax.experimental import pallas as pl
from jax.experimental.pallas import tpu as pltpu
from jax.sharding import PartitionSpec as P

GROUPS = 4
EPSILON = 1e-05
MESH = pl.DeviceIdType.MESH
F32 = jnp.float32
BF16 = jnp.bfloat16
LANES = 128
EMB_PIECES = 4
BATCHES = (((0, 1, 2), 0), ((3, 4), 0), ((5, 6, 7), 1))


def silu(x):
    return x * (1.0 / (1.0 + jnp.exp(-x)))


def softplus(x):
    return jnp.maximum(x, 0.0) + jnp.log1p(jnp.exp(-jnp.abs(x)))


def iota(shape, axis):
    return lax.broadcasted_iota(jnp.int32, shape, axis)


def keep_rows(kids, counts):
    counted = counts[0]
    for i in range(1, kids - 1):
        counted = counted + counts[i]
    running = kids - counted
    marks = [running]
    for i in range(kids - 1):
        running = running + counts[i]
        marks.append(running)
    parent = []
    for k in range(kids):
        at = jnp.int32(0)
        for mark in marks:
            at = at + (mark <= k).astype(jnp.int32)
        parent.append(jnp.minimum(at, kids - 1))
    return parent


def apart(blocks, kids):
    whole = jnp.concatenate(blocks, axis=0)
    child = iota(whole.shape, 0) % kids
    return jnp.concatenate(
        [jnp.where(child == k, whole, 0.0) for k in range(kids)], axis=1
    ).astype(BF16)


def fused(
    np_,
    nh,
    counts_h,
    step_bias_h,
    decay_log_h,
    skip_gain_h,
    tok_h,
    kern_value_h,
    bias_value_h,
    kern_wread,
    bias_wread,
    norm_gain_h,
    ssm,
    conv_value,
    conv_wread,
    emb,
    w_gate,
    w_value,
    w_wread,
    w_step,
    w_output,
    mixed_o,
    states_o,
    conv_o,
    counts,
    step_bias,
    decay_log,
    skip_gain,
    tok,
    ids_s,
    kern_value,
    bias_value,
    bw_v,
    norm_gain,
    emb_v,
    wg_v,
    wv_v,
    ww_v,
    ws_v,
    wo_v,
    win,
    cwin,
    wwin,
    kw_v,
    sbf,
    hist,
    whist,
    tok_part,
    tok_recv,
    tok_all,
    term_w,
    term_v,
    term_g,
    sib_w,
    sib_v,
    sib_g,
    out_w,
    out_v,
    out_far,
    out_near,
    in_w,
    in_v,
    in_far,
    in_near,
    quarter,
    nrm_all,
    part,
    parts,
    fin,
    conv_v,
    tok_sem,
    emb_sem,
    loc_sem,
    shift_send,
    shift_recv,
    rs_send,
    rs_recv,
    ag_send,
    ag_recv,
    sib_send,
    sib_recv,
    z_send,
    z_recv,
    far_send,
    far_recv,
    near_send,
    near_recv,
    mate_send,
    mate_recv,
    nrm_send,
    nrm_recv,
    fwd_send,
    fwd_recv,
    out_send,
    out_recv,
    res_sem,
):
    p = lax.axis_index("particle")
    h = lax.axis_index("head")
    zs = np_ // 2
    z = p // 2
    c = p % 2
    sibling = z * 2 + 1 - c
    kids = counts.shape[0]
    steps = tok.shape[0]
    own = kids * steps
    rows = np_ * own
    width = wv_v.shape[1]
    state = ssm.shape[3]
    heads = ssm.shape[1]
    headdim = ssm.shape[2]
    vocab = emb.shape[0]
    span = nh // GROUPS
    group, mate = h // span, h % span
    share = 2 * state // span
    half = rows // 2
    owned = half // nh
    reach = zs // 2
    order = [reach]
    for d in range(reach - 1, 0, -1):
        order += [d, -d]
    order.append(0)

    def chip(d):
        return lax.rem(z + d + zs, zs)

    tok_copy = pltpu.make_async_copy(tok_h, tok, tok_sem)
    tok_copy.start()
    piece = vocab // EMB_PIECES
    emb_copies = [
        pltpu.make_async_copy(
            emb.at[pl.ds(i * piece, piece)], emb_v.at[pl.ds(i * piece, piece)], emb_sem.at[i]
        )
        for i in range(EMB_PIECES)
    ]
    for copy in emb_copies:
        copy.start()

    barrier = pltpu.get_barrier_semaphore()
    mates = [{"head": lax.rem(h + j, nh)} for j in range(1, nh)]
    mates += [{"particle": lax.rem(p + 2 * j, np_)} for j in range(1, zs)]
    mates += [{"particle": sibling}, {"particle": lax.rem(p + np_ - 1 + 2 * c, np_)}]
    for other in mates:
        pl.semaphore_signal(barrier, inc=1, device_id=other, device_id_type=MESH)
    at_write = pl.ds(pl.multiple_of(group * state, state), state)
    at_read = pl.ds(pl.multiple_of((GROUPS + group) * state, state), state)
    side = mate // (span // 2)
    at_share = pl.ds(pl.multiple_of((side * GROUPS + group) * state, state), state)
    lo, hi = pl.ds(0, state), pl.ds(state, state)
    pairs = [
        (ssm.at[pl.ds(0, kids - 1)], win.at[pl.ds(1, kids - 1)]),
        (conv_value, cwin.at[1]),
        (conv_wread.at[:, :, at_write], wwin.at[1, :, :, lo]),
        (conv_wread.at[:, :, at_read], wwin.at[1, :, :, hi]),
        (counts_h, counts),
        (w_wread.at[:, at_share], ww_v),
        (w_step, ws_v),
        (w_value, wv_v),
        (w_gate, wg_v),
        (kern_wread.at[:, at_write], kw_v.at[:, lo]),
        (kern_wread.at[:, at_read], kw_v.at[:, hi]),
        (w_output, wo_v),
        (step_bias_h, step_bias),
        (decay_log_h, decay_log),
        (skip_gain_h, skip_gain),
        (kern_value_h, kern_value),
        (bias_value_h, bias_value),
        (norm_gain_h, norm_gain),
        (bias_wread.at[:, at_write], bw_v.at[:, lo]),
        (bias_wread.at[:, at_read], bw_v.at[:, hi]),
    ]
    loads = [pltpu.make_async_copy(s, d, loc_sem.at[i]) for i, (s, d) in enumerate(pairs)]

    tok_copy.wait()
    ids_t = jnp.concatenate([tok[...], jnp.zeros((8 - steps, np_ * kids), jnp.int32)], axis=0).T
    ids_s[...] = ids_t - h * vocab

    def lookup(m):
        column = []
        for d in order[m * reach : (m + 1) * reach]:
            pair = ids_s[pl.ds(pl.multiple_of(chip(d) * 2 * kids, 2 * kids), 2 * kids), :]
            for core in range(2):
                for t in range(steps):
                    column.append(pair[core * kids : (core + 1) * kids, t : t + 1])
        ids = jnp.concatenate(column, axis=0)
        total = None
        for i in range(EMB_PIECES):
            if m == 0:
                emb_copies[i].wait()
            hot = jnp.where(ids - i * piece == iota((half, piece), 1), 1.0, 0.0).astype(BF16)
            term = jnp.dot(hot, emb_v[pl.ds(i * piece, piece)], preferred_element_type=F32)
            total = term if total is None else total + term
        tok_part[m] = total.astype(BF16).reshape(nh, owned, -1)

    side_x = math.isqrt(nh)
    side_y = nh // side_x
    offsets = [(a, b) for a in range(side_x) for b in range(side_y) if a or b]
    offsets.sort(key=lambda o: -min(o[0], side_x - o[0]) - min(o[1], side_y - o[1]))

    def at_offset(j, way):
        a, b = offsets[j - 1]
        x = lax.rem(h // side_y + way * a + side_x, side_x)
        y = lax.rem(h % side_y + way * b + side_y, side_y)
        return x * side_y + y

    def rs_copy(m, j):
        dest = at_offset(j, 1)
        return pltpu.make_async_remote_copy(
            src_ref=tok_part.at[m, dest],
            dst_ref=tok_recv.at[m, j - 1],
            send_sem=rs_send.at[m, j - 1],
            recv_sem=rs_recv.at[m, j - 1],
            device_id={"head": dest},
            device_id_type=MESH,
        )

    def ag_copy(m, j):
        return pltpu.make_async_remote_copy(
            src_ref=tok_all.at[m, h],
            dst_ref=tok_all.at[m, h],
            send_sem=ag_send.at[m, j - 1],
            recv_sem=ag_recv.at[m, j - 1],
            device_id={"head": at_offset(j, 1)},
            device_id_type=MESH,
        )

    def ag_back(m, j):
        source = at_offset(j, -1)
        return pltpu.make_async_remote_copy(
            src_ref=tok_all.at[m, h],
            dst_ref=tok_all.at[m, source],
            send_sem=ag_send.at[m, j - 1],
            recv_sem=ag_recv.at[m, j - 1],
            device_id={"head": source},
            device_id_type=MESH,
        )

    def each(do):
        for j in range(1, nh):
            do(j)

    lookup(0)
    pl.semaphore_wait(barrier, len(mates))
    each(lambda j: rs_copy(0, j).start())
    lookup(1)
    each(lambda j: rs_copy(1, j).start())
    for copy in loads:
        copy.start()

    above = lax.rem(p + 1, np_)
    shift_pairs = [
        (ssm.at[kids - 1], win.at[0]),
        (conv_value, cwin.at[0]),
        (conv_wread.at[:, :, at_write], wwin.at[0, :, :, lo]),
        (conv_wread.at[:, :, at_read], wwin.at[0, :, :, hi]),
    ]
    shifts = [
        pltpu.make_async_remote_copy(
            src_ref=s,
            dst_ref=d,
            send_sem=shift_send.at[i],
            recv_sem=shift_recv.at[i],
            device_id={"particle": above},
            device_id_type=MESH,
        )
        for i, (s, d) in enumerate(shift_pairs)
    ]
    for copy in shifts:
        copy.start()

    for m in range(2):
        shared = tok_part[m, h]
        for j in reversed(range(1, nh)):
            rs_copy(m, j).wait_recv()
            shared = shared + tok_recv[m, j - 1]
        tok_all[m, h] = shared
        each(lambda j, m=m: ag_copy(m, j).start())

    for copy in loads[:5]:
        copy.wait()
    parent = keep_rows(kids, counts)
    for copy in shifts:
        copy.wait_recv()
    for k in range(kids):
        sbf[:, pl.ds(k * state, state)] = win[parent[k]].reshape(width, state).astype(BF16)
        here = jnp.minimum(parent[k], 1)
        row = pl.ds(jnp.where(parent[k] == 0, kids - 1, parent[k] - 1), 1)
        for tap in range(3):
            hist[tap, pl.ds(k, 1), :] = cwin[here, tap, row, :]
            whist[tap, pl.ds(k, 1), :] = wwin[here, tap, row, :]
    for copy in loads[5:]:
        copy.wait()

    kinds = [
        (term_w, sib_w, out_w, in_w),
        (term_v, sib_v, out_v, in_v),
        (term_g, sib_g),
    ]

    def sib_copy(kind, m):
        source, target = kinds[kind][:2]
        return pltpu.make_async_remote_copy(
            src_ref=source.at[1 - c, pl.ds(m * reach, reach)],
            dst_ref=target.at[pl.ds(m * reach, reach)],
            send_sem=sib_send.at[kind, m],
            recv_sem=sib_recv.at[kind, m],
            device_id={"particle": sibling},
            device_id_type=MESH,
        )

    def along(d):
        return {"particle": lax.rem(p + 2 * d + np_, np_)}

    def z_copy(kind, i):
        _, _, out, back = kinds[kind]
        return pltpu.make_async_remote_copy(
            src_ref=out.at[i],
            dst_ref=back.at[i],
            send_sem=z_send.at[kind, i],
            recv_sem=z_recv.at[kind, i],
            device_id=along(order[i]),
            device_id_type=MESH,
        )

    def place(kind, m, terms):
        source = kinds[kind][0]
        for b in range(2 * reach):
            block = terms[b * own : (b + 1) * own].astype(BF16)
            source[b % 2, m * reach + b // 2] = block.reshape(source.shape[2:])
        sib_copy(kind, m).start()

    def chip_sum(kind, i):
        return kinds[kind][0][c, i].astype(F32) + kinds[kind][1][i].astype(F32)

    def send_sums(kind, which):
        for i in which:
            kinds[kind][2][i] = chip_sum(kind, i).astype(BF16)
            z_copy(kind, i).start()

    def arrive(kind):
        total = chip_sum(kind, zs - 1)
        for i in range(zs - 1):
            z_copy(kind, i).wait_recv()
            total = total + kinds[kind][3][i].astype(F32)
        return total.astype(BF16)

    def gate_sum(d, q):
        i = order.index(d)
        return term_g[c, i, q].astype(F32) + sib_g[i, q].astype(F32)

    def whole(q, way):
        return (way == 1) == (q == 0)

    def far_copy(q, way):
        side = (1 - way) // 2
        cut = pl.ds(0, 2) if whole(q, way) else pl.ds(1, 1)
        return pltpu.make_async_remote_copy(
            src_ref=out_far.at[q, side, cut],
            dst_ref=in_far.at[q, side, cut],
            send_sem=far_send.at[q, side],
            recv_sem=far_recv.at[q, side],
            device_id=along(2 * way),
            device_id_type=MESH,
        )

    def near_copy(q, way, n):
        side = (1 - way) // 2
        return pltpu.make_async_remote_copy(
            src_ref=out_near.at[q, side, n],
            dst_ref=in_near.at[q, side, n],
            send_sem=near_send.at[q, side, n],
            recv_sem=near_recv.at[q, side, n],
            device_id=along((2 - n) * way),
            device_id_type=MESH,
        )

    legs = [(q, way) for q in range(2) for way in (1, -1)]

    for m in range(2):
        each(lambda j, m=m: ag_back(m, j).wait_recv())
        tokens = tok_all[m].reshape(half, -1)
        place(2, m, jnp.dot(tokens, wg_v[...], preferred_element_type=F32))
        matrices = jnp.dot(tokens, ww_v[...], preferred_element_type=F32)
        rate = lax.dot_general(
            tokens, ws_v[...], (((1,), (1,)), ((), ())), preferred_element_type=F32
        )
        pads = [jnp.zeros((half, n), F32) for n in (share, LANES - share - heads)]
        rate = jnp.concatenate([pads[0], rate, pads[1]], axis=1)
        turned = jnp.concatenate([matrices[:, share:], matrices[:, :share]], axis=1)
        matrices = jnp.where(mate % (span // 2) == 0, matrices, turned)
        place(0, m, jnp.where(iota((half, LANES), 1) < share, matrices, rate))
        sib_copy(2, m).wait_recv()
        if m == 0:
            for q, way in legs:
                side = (1 - way) // 2
                if whole(q, way):
                    out_far[q, side, 0] = gate_sum(reach, q).astype(BF16)
                out_far[q, side, 1] = gate_sum(way * (reach - 1), q).astype(BF16)
                far_copy(q, way).start()
        place(1, m, jnp.dot(tokens, wv_v[...], preferred_element_type=F32))
        sib_copy(0, m).wait_recv()
        send_sums(0, range(m * reach, min((m + 1) * reach, zs - 1)))
        sib_copy(1, m).wait_recv()
    send_sums(1, range(zs - 1))
    for q, way in legs:
        side = (1 - way) // 2
        far_copy(q, way).wait_recv()
        for n in range(2):
            term = gate_sum(way * (2 - n), q)
            if n == 1 or whole(q, way):
                term = term + in_far[q, side, n].astype(F32)
            out_near[q, side, n] = term.astype(BF16)
            near_copy(q, way, n).start()

    def arrive_gate(q):
        total = gate_sum(0, q)
        for side, way in enumerate((1, -1)):
            for n in range(2):
                near_copy(q, way, n).wait_recv()
                total = total + in_near[q, side, n].astype(F32)
        return total.astype(BF16)

    narrow = arrive(0)
    quarter[mate] = narrow

    def mate_copy(j):
        return pltpu.make_async_remote_copy(
            src_ref=quarter.at[mate],
            dst_ref=quarter.at[mate],
            send_sem=mate_send.at[j - 1],
            recv_sem=mate_recv.at[j - 1],
            device_id={"head": group * span + lax.rem(mate + j, span)},
            device_id_type=MESH,
        )

    def mate_back(j):
        source = lax.rem(mate + span - j, span)
        return pltpu.make_async_remote_copy(
            src_ref=quarter.at[mate],
            dst_ref=quarter.at[source],
            send_sem=mate_send.at[j - 1],
            recv_sem=mate_recv.at[j - 1],
            device_id={"head": group * span + source},
            device_id_type=MESH,
        )

    for j in range(1, span):
        mate_copy(j).start()

    def at_step(a, t):
        return a[t * kids : (t + 1) * kids]

    spread = (
        iota((LANES, width), 1) // headdim + share == iota((LANES, width), 0)
    ).astype(F32)
    rates = jnp.dot(narrow, spread.astype(BF16), preferred_element_type=F32)
    lane_head = iota((1, width), 1) // headdim

    def per_head(ref):
        out = jnp.zeros((1, width), F32)
        for i in range(heads):
            out = jnp.where(lane_head == i, ref[i], out)
        return out

    step_size = softplus(rates + per_head(step_bias))
    decay = jnp.exp(-step_size * jnp.exp(per_head(decay_log)))
    skip = per_head(skip_gain)

    def convolve(past, current, kern, bias):
        seq = [past[i] for i in range(3)] + [at_step(current, t) for t in range(steps)]
        out = []
        for t in range(steps):
            a = seq[t] * kern[0:1]
            for i in range(1, 4):
                a = a + seq[t + i] * kern[i : i + 1]
            out.append(silu(a + bias))
        return out

    for j in range(1, span):
        mate_back(j).wait_recv()
    wread = jnp.concatenate([quarter[i].astype(F32)[:, :share] for i in range(span)], axis=1)
    conv_w = convolve(whist, wread, kw_v[...], bw_v[...])
    writes = [a[:, :state] for a in conv_w]
    reads = [a[:, state:] for a in conv_w]
    first = lax.dot_general(
        apart(reads, kids), sbf[...], (((1,), (1,)), ((), ())), preferred_element_type=F32
    )
    kept = None
    starts = []
    for t in range(steps):
        now = at_step(decay, t)
        kept = now if kept is None else kept * now
        starts.append(kept * at_step(first, t))
    match = {
        (u, t): jnp.sum(writes[u] * reads[t], axis=1, keepdims=True)
        for t in range(steps)
        for u in range(t + 1)
    }
    value = arrive(1).astype(F32)
    conv = convolve(hist, value, kern_value[...], bias_value[...])

    added = []
    readings = []
    for t in range(steps):
        now = at_step(decay, t)
        added = [a * now for a in added] + [at_step(step_size, t) * conv[t]]
        reading = starts[t] + skip * conv[t]
        for u in range(t + 1):
            reading = reading + added[u] * match[u, t]
        readings.append(reading)
    gate = jnp.concatenate([arrive_gate(q) for q in range(2)], axis=0).astype(F32)
    gated = jnp.concatenate(readings, axis=0) * silu(gate)

    scaled = (gated * norm_gain[...]).astype(BF16)
    at_row, from_row = iota((own, own), 0), iota((own, own), 1)
    turn = (from_row == (at_row % steps) * kids + at_row // steps).astype(F32).astype(BF16)
    scaled = jnp.dot(turn, scaled, preferred_element_type=F32)
    bands, cuts = own // 16, width // LANES
    for r in range(bands):
        for i in range(cuts):
            tile = scaled[r * 16 : (r + 1) * 16, i * LANES : (i + 1) * LANES]
            nrm_all[p, r * cuts + i] = tile.astype(BF16)

    def nrm_copy(at, target, send, recv):
        return pltpu.make_async_remote_copy(
            src_ref=nrm_all.at[at],
            dst_ref=nrm_all.at[at],
            send_sem=send,
            recv_sem=recv,
            device_id={"particle": target},
            device_id_type=MESH,
        )

    def direct(i):
        target = lax.rem(p + 2 * order[i] + np_, np_)
        return nrm_copy(p, target, nrm_send.at[i], nrm_recv.at[i])

    def forward(i):
        at = lax.rem(p - 2 * order[i] + np_, np_)
        return nrm_copy(at, sibling, fwd_send.at[i], fwd_recv.at[i])

    for i in reversed(range(zs - 1)):
        direct(i).start()
    forward(zs - 1).start()

    def dest_of(i, other):
        return chip(-order[i]) * 2 + (1 - c if other else c)

    def out_copy(i, other):
        return pltpu.make_async_remote_copy(
            src_ref=part.at[i, other],
            dst_ref=parts.at[h],
            send_sem=out_send.at[i, other],
            recv_sem=out_recv.at[h],
            device_id={"head": dest_of(i, other)},
            device_id_type=MESH,
        )

    def send_parts(places):
        block = []
        for i, other in places:
            tiles = nrm_all[dest_of(i, other)]
            for r in range(bands):
                block.append(
                    jnp.concatenate([tiles[r * cuts + n] for n in range(cuts)], axis=1)
                )
        block = jnp.concatenate(block, axis=0)
        product = jnp.dot(block, wo_v[...], preferred_element_type=F32).astype(BF16)
        plain = block.astype(F32) * ungain
        squares = jnp.sum(plain * plain, axis=1, keepdims=True)
        upper = squares.astype(BF16).astype(F32)
        lane = iota((block.shape[0], LANES), 1)
        squares = jnp.where(lane % 2 == 0, upper, squares - upper)
        for n, (i, other) in enumerate(places):
            marks = squares[n * own : n * own + 16]
            for r in range(1, bands):
                start = n * own + r * 16
                marks = jnp.where(lane[:16] < 2 * r, marks, squares[start : start + 16])
            part[i, other, bands * cuts] = marks.astype(BF16)
            for r in range(bands):
                start = n * own + r * 16
                for e in range(cuts):
                    part[i, other, r * cuts + e] = product[
                        start : start + 16, e * LANES : (e + 1) * LANES
                    ]
        for i, other in places:
            dest = dest_of(i, other)

            @pl.when(dest != h)
            def _(i=i, other=other):
                out_copy(i, other).start()

            @pl.when(dest == h)
            def _(i=i, other=other):
                parts[h] = part[i, other]

    def take(i):
        at = chip(-order[i]) * 2 + c
        if order[i] != 0:
            nrm_copy(at, sibling, nrm_send.at[i], nrm_recv.at[i]).wait_recv()
            forward(i).start()

    def take_forward(i):
        at = chip(-order[i]) * 2 + 1 - c
        nrm_copy(at, sibling, fwd_send.at[i], fwd_recv.at[i]).wait_recv()

    ungain = 1.0 / norm_gain[...]
    near = list(range(zs))[::-1]
    for batch, split in BATCHES:
        batch = [near[n] for n in batch]
        for i in batch:
            take(i)
        if split:
            send_parts([(i, 0) for i in batch])
        for i in batch:
            take_forward(i)
        send_parts([(i, o) for i in batch for o in range(split, 2)])

    adds = lax.dot_general(
        jnp.concatenate(added, axis=0).astype(BF16),
        apart(writes, kids),
        (((0,), (0,)), ((), ())),
        preferred_element_type=F32,
    )
    for k in range(kids):
        for i in range(heads):
            factor = jnp.broadcast_to(
                kept[k : k + 1, i * headdim : i * headdim + 1], (headdim, state)
            )
            fin[k, i] = (
                win[parent[k], i] * factor
                + adds[i * headdim : (i + 1) * headdim, k * state : (k + 1) * state]
            )
    for i in range(3):
        conv_v[i] = at_step(value, steps - 3 + i)
    results = [
        pltpu.make_async_copy(s, d, res_sem.at[i])
        for i, (s, d) in enumerate([(fin, states_o), (conv_v, conv_o)])
    ]
    for copy in results:
        copy.start()

    for m in range(2):
        each(lambda j, m=m: rs_copy(m, j).wait_send())
        each(lambda j, m=m: ag_copy(m, j).wait_send())
    for copy in shifts:
        copy.wait_send()
    for kind in range(3):
        for m in range(2):
            sib_copy(kind, m).wait_send()
    for kind in range(2):
        for i in range(zs - 1):
            z_copy(kind, i).wait_send()
    for q, way in legs:
        far_copy(q, way).wait_send()
        for n in range(2):
            near_copy(q, way, n).wait_send()
    for j in range(1, span):
        mate_copy(j).wait_send()
    for i in range(zs - 1):
        direct(i).wait_send()
    for i in range(zs):
        forward(i).wait_send()
    for copy in results:
        copy.wait()

    totals = [[jnp.zeros((16, LANES), F32) for _ in range(cuts)] for _ in range(bands)]
    for g in range(GROUPS):
        sums = [[jnp.zeros((16, LANES), F32) for _ in range(cuts)] for _ in range(bands)]
        squares = [jnp.zeros((16, 1), F32) for _ in range(bands)]
        for s in range(g * span, (g + 1) * span):

            @pl.when(s != h)
            def _(s=s):
                pltpu.make_async_remote_copy(
                    src_ref=part.at[0, 0],
                    dst_ref=parts.at[s],
                    send_sem=out_send.at[0, 0],
                    recv_sem=out_recv.at[s],
                    device_id={"head": s},
                    device_id_type=MESH,
                ).wait_recv()

            marks = parts[s, bands * cuts].astype(F32)
            for r in range(bands):
                squares[r] = squares[r] + marks[:, 2 * r : 2 * r + 1] + marks[:, 2 * r + 1 : 2 * r + 2]
                for e in range(cuts):
                    sums[r][e] = sums[r][e] + parts[s, r * cuts + e].astype(F32)
        for r in range(bands):
            scale = lax.rsqrt(squares[r] / (width * span) + EPSILON)
            totals[r] = [a + b * scale for a, b in zip(totals[r], sums[r])]
    for r in range(bands):
        answer = jnp.concatenate(totals[r], axis=1)
        each_kid = 16 // steps
        for k in range(each_kid):
            mixed_o[r * each_kid + k] = answer[k * steps : (k + 1) * steps].astype(BF16)
    for i in range(zs):
        for other in range(2):

            @pl.when(dest_of(i, other) != h)
            def _(i=i, other=other):
                out_copy(i, other).wait_send()


def finish(mixed, states, conv, mixed_o, states_o, conv_o, sems):
    pairs = [(states.at[k], states_o.at[k]) for k in range(states.shape[0])]
    pairs += [(mixed, mixed_o), (conv, conv_o)]
    copies = [pltpu.make_async_copy(a, b, sems.at[i]) for i, (a, b) in enumerate(pairs)]
    for copy in copies:
        copy.start()
    for copy in copies:
        copy.wait()


def on_device(
    np_,
    nh,
    counts,
    ssm_state,
    conv_value,
    conv_wread,
    token_ids,
    embedding,
    w_gate,
    w_value,
    w_wread,
    w_step,
    kern_value,
    bias_value,
    kern_wread,
    bias_wread,
    step_bias,
    decay_log,
    skip_gain,
    norm_gain,
    w_output,
):
    kids, heads, headdim, state = ssm_state.shape
    steps = token_ids.shape[1]
    own = kids * steps
    rows = np_ * own
    owned = rows // 2 // nh
    depth, width = w_value.shape
    cols = w_output.shape[1]
    zs = np_ // 2
    span = nh // GROUPS
    taps = kern_value.shape[0]
    tiles = own // 16 * (width // LANES) + 1
    dma = pltpu.SemaphoreType.DMA
    smem = pltpu.SMEM
    vmem = pltpu.VMEM
    scratch = [
        smem((kids,), jnp.int32),
        smem((heads,), F32),
        smem((heads,), F32),
        smem((heads,), F32),
        vmem((steps, np_ * kids), jnp.int32),
        vmem((np_ * kids, 8), jnp.int32),
        vmem((taps, width), F32),
        vmem((1, width), F32),
        vmem((1, 2 * state), F32),
        vmem((1, width), F32),
        vmem(embedding.shape, BF16),
        vmem((depth, width), BF16),
        vmem((depth, width), BF16),
        vmem((depth, state), BF16),
        vmem((heads, depth), BF16),
        vmem((width, cols), BF16),
        vmem((kids, heads, headdim, state), F32),
        vmem((2, 3, kids, width), F32),
        vmem((2, 3, kids, 2 * state), F32),
        vmem((taps, 2 * state), F32),
        vmem((width, kids * state), BF16),
        vmem((3, kids, width), F32),
        vmem((3, kids, 2 * state), F32),
        vmem((2, nh, owned, depth), BF16),
        vmem((2, nh - 1, owned, depth), BF16),
        vmem((2, nh, owned, depth), BF16),
        vmem((2, zs, own, LANES), BF16),
        vmem((2, zs, own, width), BF16),
        vmem((2, zs, 2, own // 2, width), BF16),
        vmem((zs, own, LANES), BF16),
        vmem((zs, own, width), BF16),
        vmem((zs, 2, own // 2, width), BF16),
        vmem((zs - 1, own, LANES), BF16),
        vmem((zs - 1, own, width), BF16),
        vmem((2, 2, 2, own // 2, width), BF16),
        vmem((2, 2, 2, own // 2, width), BF16),
        vmem((zs - 1, own, LANES), BF16),
        vmem((zs - 1, own, width), BF16),
        vmem((2, 2, 2, own // 2, width), BF16),
        vmem((2, 2, 2, own // 2, width), BF16),
        vmem((span, own, LANES), BF16),
        vmem((np_, tiles - 1, 16, LANES), BF16),
        vmem((zs, 2, tiles, 16, LANES), BF16),
        vmem((nh, tiles, 16, LANES), BF16),
        vmem(ssm_state.shape, F32),
        vmem((3, kids, width), F32),
        dma,
        dma((EMB_PIECES,)),
        dma((20,)),
        dma((4,)),
        dma((4,)),
        dma((2, nh - 1)),
        dma((2, nh - 1)),
        dma((2, nh - 1)),
        dma((2, nh - 1)),
        dma((3, 2)),
        dma((3, 2)),
        dma((2, zs - 1)),
        dma((2, zs - 1)),
        dma((2, 2)),
        dma((2, 2)),
        dma((2, 2, 2)),
        dma((2, 2, 2)),
        dma((span - 1,)),
        dma((span - 1,)),
        dma((zs - 1,)),
        dma((zs - 1,)),
        dma((zs,)),
        dma((zs,)),
        dma((zs, 2)),
        dma((nh,)),
        dma((2,)),
    ]
    hbm = pl.BlockSpec(memory_space=pltpu.HBM)
    limit = 40 * 1024 * 1024
    shape = jax.ShapeDtypeStruct
    operands = (        counts,
        step_bias,
        decay_log,
        skip_gain,
        token_ids.T,
        kern_value,
        bias_value.reshape(1, -1),
        kern_wread,
        bias_wread.reshape(1, -1),
        norm_gain.reshape(1, -1),
        ssm_state,
        conv_value.transpose(1, 0, 2),
        conv_wread.transpose(1, 0, 2),
        embedding,
        w_gate,
        w_value,
        w_wread,
        w_step.T,
        w_output,
    )
    operands = [pltpu.with_memory_space_constraint(a, pltpu.HBM) for a in operands]
    results = pl.pallas_call(
        functools.partial(fused, np_, nh),
        out_shape=(
            shape((kids, steps, cols), BF16),
            shape(ssm_state.shape, F32),
            shape((3, kids, width), F32),
        ),
        in_specs=[hbm] * 19,
        out_specs=(pl.BlockSpec(memory_space=pltpu.VMEM),)
        + (pl.BlockSpec(memory_space=pl.ANY),) * 2,
        scratch_shapes=scratch,
        compiler_params=pltpu.CompilerParams(
            collective_id=0, has_side_effects=True, vmem_limit_bytes=limit
        ),
    )(*operands)
    mixed, final_state, final_conv = pl.pallas_call(
        finish,
        out_shape=(
            shape((kids, steps, cols), BF16),
            shape(ssm_state.shape, F32),
            shape((3, kids, width), F32),
        ),
        in_specs=[pl.BlockSpec(memory_space=pltpu.VMEM)] * 3,
        out_specs=(hbm,) * 3,
        scratch_shapes=[dma((kids + 2,))],
        compiler_params=pltpu.CompilerParams(vmem_limit_bytes=limit),
    )(*results)
    return mixed, final_state, final_conv.transpose(1, 0, 2)


def solution(mesh):
    return jax.shard_map(
        functools.partial(on_device, mesh.shape["particle"], mesh.shape["head"]),
        mesh=mesh,
        in_specs=(
            P("particle"),
            P("particle", "head", None, None),
            P("particle", None, "head"),
            P("particle", None, None),
            P(),
            P("head", "particle"),
            P("particle", "head"),
            P("particle", "head"),
            P("particle", None),
            P("particle", "head"),
            P(None, "head"),
            P("head"),
            P(),
            P(),
            P("head"),
            P("head"),
            P("head"),
            P("head"),
            P("head", "particle"),
        ),
        out_specs=(
            P("head", None, "particle"),
            P("particle", "head", None, None),
            P("particle", None, "head"),
        ),
        check_vma=False,
    )
```
